128 devices in a mesh: ctx: 64 (over x_lo, z, y, core), fsdp: 2 (over x_hi).
Axes of the slice: x: 4 (x_hi: 2, x_lo: 2; x = x_hi * 2 + x_lo), y: 4, z: 4, core: 2. Of those that a mesh axis runs over, the one named last changes fastest.
Arguments:
- inputs: bfloat16 [2, 8192, 640], P('fsdp', 'ctx'), may hold values from -6 to 6
- pair_order: int32 [64], replicated, may hold values from 0 to 63, each once
- w_query: bfloat16 [640, 1024], P('fsdp'), may hold values from -0.25 to 0.25
- w_key: bfloat16 [640, 256], P('fsdp'), may hold values from -0.25 to 0.25
- w_value: bfloat16 [640, 256], P('fsdp'), may hold values from -0.25 to 0.25
- w_output: bfloat16 [1024, 640], P('fsdp'), may hold values from -0.1875 to 0.1875
- w_gate: bfloat16 [640, 2048], P('fsdp'), may hold values from -0.25 to 0.25
- w_up: bfloat16 [640, 2048], P('fsdp'), may hold values from -0.25 to 0.25
- w_down: bfloat16 [2048, 640], P('fsdp'), may hold values from -0.125 to 0.125
- gain_in: float32 [640], replicated, may hold values from 0.25 to 1.75
- gain_query: float32 [256], replicated, may hold values from 0.25 to 1.75
- gain_key: float32 [256], replicated, may hold values from 0.25 to 1.75
- gain_post_attn: float32 [640], replicated, may hold values from 0.25 to 1.75
- gain_pre_ff: float32 [640], replicated, may hold values from 0.25 to 1.75
- gain_post_ff: float32 [640], replicated, may hold values from 0.25 to 1.75
- cotangent: bfloat16 [2, 8192, 640], P('fsdp', 'ctx'), may hold values from -6 to 6
Outputs:
- layer_out: bfloat16 [2, 8192, 640], P('fsdp', 'ctx')
- input_grad: bfloat16 [2, 8192, 640], P('fsdp', 'ctx')
- grad_query: float32 [640, 1024], P(('ctx', 'fsdp'))
- grad_key: float32 [640, 256], P(('ctx', 'fsdp'))
- grad_value: float32 [640, 256], P(('ctx', 'fsdp'))
- grad_output: float32 [1024, 640], P(('ctx', 'fsdp'))
- grad_gate: float32 [640, 2048], P(('ctx', 'fsdp'))
- grad_up: float32 [640, 2048], P(('ctx', 'fsdp'))
- grad_down: float32 [2048, 640], P(('ctx', 'fsdp'))
- grad_gain_in: float32 [640], P(('ctx', 'fsdp'))
- grad_gain_query: float32 [256], P(('ctx', 'fsdp'))
- grad_gain_key: float32 [256], P(('ctx', 'fsdp'))
- grad_gain_post_attn: float32 [640], P(('ctx', 'fsdp'))
- grad_gain_pre_ff: float32 [640], P(('ctx', 'fsdp'))
- grad_gain_post_ff: float32 [640], P(('ctx', 'fsdp'))
The draws below stay inside these ranges and needn't reach their ends.
Inputs may be any that keep to these rules, and one draw needn't show every extreme that they name: Index i of ctx holds blocks pair_order[i] and 127 - pair_order[i] of every sequence, 64 tokens each, in that order; every pair is held once.
All inputs are finite; a program needn't handle non-finite values.
Results may differ from the reference program's by a relative error of at most 0.038.
Values may be sent and summed in bfloat16 or wider, within the bound.
A program may use at most 128 MiB of HBM per device.

```python
import math
import jax
import jax.numpy as jnp
from jax import lax

D = 640
FF = 2048
HEADS = 4
HD = 256
BLK = 64
QDIM = 1024
LEN = 8192
SEQS = 2
N_CTX = 64


def block_scale(key, dims, cuts, smallest, top_value):
    loudness, own = 1.0, jax.random.fold_in(key, 6)
    for dim, parts in cuts:
        draws = jnp.exp(jax.random.uniform(jax.random.fold_in(own, dim), (parts,), jnp.float32, smallest / len(cuts), top_value / len(cuts)))
        loudness = loudness * jnp.repeat(draws, dims[dim] // parts).reshape([-1 if axis == dim else 1 for axis in range(len(dims))])
    return loudness


def bell_draw(stream_key, extent, deviation, limit, split=(), held_as=jnp.bfloat16):
    level = block_scale(stream_key, extent, split, -0.22, 0.18) if split else 1.0
    array = jax.random.normal(stream_key, extent, jnp.float32) * deviation * level
    return jnp.minimum(jnp.maximum(array, -limit), limit).astype(held_as)


def setup_inputs(seed: int = 0) -> dict:
    arg_keys = jax.random.split(jax.random.key(seed), 17)
    return {
        "inputs": bell_draw(arg_keys[0], (SEQS, LEN, D), 1.0, 6.0, ((0, 2), (1, 64))),
        "pair_order": jax.random.permutation(arg_keys[1], N_CTX).astype(jnp.int32),
        "w_query": bell_draw(arg_keys[2], (D, QDIM), D ** -0.5, 0.25, ((0, 2),)),
        "w_key": bell_draw(arg_keys[3], (D, HD), D ** -0.5, 0.25, ((0, 2),)),
        "w_value": bell_draw(arg_keys[4], (D, HD), D ** -0.5, 0.25, ((0, 2),)),
        "w_output": bell_draw(arg_keys[5], (QDIM, D), QDIM ** -0.5, 0.1875, ((0, 2),)),
        "w_gate": bell_draw(arg_keys[6], (D, FF), D ** -0.5, 0.25, ((0, 2),)),
        "w_up": bell_draw(arg_keys[7], (D, FF), D ** -0.5, 0.25, ((0, 2),)),
        "w_down": bell_draw(arg_keys[8], (FF, D), FF ** -0.5, 0.125, ((0, 2),)),
        "gain_in": jnp.clip(1.0 + 0.15 * jax.random.normal(arg_keys[9], (D,), jnp.float32), 0.25, 1.75),
        "gain_query": jnp.clip(1.0 + 0.15 * jax.random.normal(arg_keys[10], (HD,), jnp.float32), 0.25, 1.75),
        "gain_key": jnp.clip(1.0 + 0.15 * jax.random.normal(arg_keys[11], (HD,), jnp.float32), 0.25, 1.75),
        "gain_post_attn": jnp.clip(1.0 + 0.15 * jax.random.normal(arg_keys[12], (D,), jnp.float32), 0.25, 1.75),
        "gain_pre_ff": jnp.clip(1.0 + 0.15 * jax.random.normal(arg_keys[13], (D,), jnp.float32), 0.25, 1.75),
        "gain_post_ff": jnp.clip(1.0 + 0.15 * jax.random.normal(arg_keys[14], (D,), jnp.float32), 0.25, 1.75),
        "cotangent": bell_draw(arg_keys[15], (SEQS, LEN, D), 1.0, 6.0, ((0, 2), (1, 64))),
    }


EPS = 1e-06
ROPE_BASE = 1000000.0
SCALE = 0.0625
MASKED = -1e+30

@jax.custom_vjp
def low(v):
    return lax.optimization_barrier(v.astype(jnp.bfloat16)).astype(jnp.float32)

@jax.custom_vjp
def low_back(v):
    return v

def low_keep(v):
    return (low(v), None)

def low_pass(kept, grad):
    return (grad,)

def back_keep(v):
    return (v, None)

def back_low(kept, grad):
    return (low(grad),)
low.defvjp(low_keep, low_pass)
low_back.defvjp(back_keep, back_low)

def norm_scale(values, gain):
    return values * lax.rsqrt(lax.optimization_barrier(jnp.mean(values * values, axis=-1, keepdims=True)) + EPS) * gain

def rotate(values, angles):
    half = values.shape[-1] // 2
    first = values[..., :half]
    second = values[..., half:]
    cosine = jnp.cos(angles)
    sine = jnp.sin(angles)
    return jnp.concatenate([first * cosine - second * sine, second * cosine + first * sine], axis=-1)

def positions_of(pair_order, count):
    rows = jnp.arange(count, dtype=jnp.int32)
    device = rows // (2 * BLK)
    within = rows % (2 * BLK)
    pair = jnp.take(pair_order, device)
    block_id = jnp.where(within < BLK, pair, 2 * N_CTX - 1 - pair)
    return (block_id * BLK + within % BLK).astype(jnp.int32)

def matmul(left, right):
    return jnp.dot(left, right, precision=lax.Precision.HIGHEST, preferred_element_type=jnp.float32)

def layer(states, w_query, w_key, w_value, w_output, w_gate, w_up, w_down, gain_in, gain_query, gain_key, gain_post_attn, gain_pre_ff, gain_post_ff, positions):
    half = HD // 2
    freq = ROPE_BASE ** (-jnp.arange(half, dtype=jnp.float32) / half)
    angles = positions.astype(jnp.float32)[:, None] * freq
    act_one = low(norm_scale(states, gain_in))
    query_lin = low_back(matmul(act_one, w_query))
    key_lin = low_back(matmul(act_one, w_key))
    value = low_back(low(matmul(act_one, w_value)))
    query = low(rotate(norm_scale(query_lin.reshape(LEN, HEADS, HD), gain_query), angles[:, None, :]))
    key = low(rotate(norm_scale(key_lin, gain_key), angles))
    qblock = math.gcd(512, LEN)
    query_blocks = query.reshape(LEN // qblock, qblock, HEADS, HD)
    pos_blocks = positions.reshape(LEN // qblock, qblock)

    def attend(pair):
        qpart, qpos = pair
        scores = jnp.einsum('bhd,kd->bhk', qpart, key, precision=lax.Precision.HIGHEST) * SCALE
        scores = low_back(scores)
        visible = positions[None, None, :] <= qpos[:, None, None]
        scores = jnp.where(visible, scores, MASKED)
        top = lax.optimization_barrier(jnp.max(scores, axis=-1, keepdims=True))
        expo = jnp.exp(scores - top)
        probs = expo / lax.optimization_barrier(jnp.sum(expo, axis=-1, keepdims=True))
        return jnp.einsum('bhk,kd->bhd', low(probs), value, precision=lax.Precision.HIGHEST)
    attended = lax.map(jax.checkpoint(attend), (query_blocks, pos_blocks)).reshape(LEN, HEADS * HD)
    attended = low_back(low(attended))
    att_lin = low_back(matmul(attended, w_output))
    resid = states + norm_scale(att_lin, gain_post_attn)
    act_two = low(norm_scale(resid, gain_pre_ff))
    gate = low_back(matmul(act_two, w_gate))
    upper = low_back(matmul(act_two, w_up))
    hidden = low(jax.nn.gelu(gate, approximate=True) * upper)
    down = low_back(matmul(hidden, w_down))
    return resid + norm_scale(down, gain_post_ff)

def reference(inputs, pair_order, w_query, w_key, w_value, w_output, w_gate, w_up, w_down, gain_in, gain_query, gain_key, gain_post_attn, gain_pre_ff, gain_post_ff, cotangent):
    positions = positions_of(pair_order, LEN)
    params = tuple((p.astype(jnp.float32) for p in (w_query, w_key, w_value, w_output, w_gate, w_up, w_down, gain_in, gain_query, gain_key, gain_post_attn, gain_pre_ff, gain_post_ff)))

    def one_sequence(totals, pair):
        states, cot = pair
        result, pullback = jax.vjp(lambda *values: layer(*values, positions), states.astype(jnp.float32), *params)
        grads = pullback(cot.astype(jnp.float32))
        totals = tuple((t + g for t, g in zip(totals, grads[1:])))
        return (totals, (result.astype(jnp.bfloat16), grads[0].astype(jnp.bfloat16)))
    start = tuple((jnp.zeros_like(p) for p in params))
    totals, (outputs, in_grads) = lax.scan(one_sequence, start, (inputs, cotangent))
    return (outputs, in_grads, totals[0], totals[1], totals[2], totals[3], totals[4], totals[5], totals[6], totals[7], totals[8], totals[9], totals[10], totals[11], totals[12])
```

```python
import functools
import math

import jax
import jax.numpy as jnp
from jax import lax
from jax.experimental import pallas as pl
from jax.experimental.pallas import tpu as pltpu
from jax.sharding import PartitionSpec as P

EPS = 1e-06
ROPE_BASE = 1000000.0
SCALE = 0.0625
EXP2_SCALE = SCALE * math.log2(math.e)
MESH = pl.DeviceIdType.MESH
BF16 = jnp.bfloat16
F32 = jnp.float32
ANY = pl.BlockSpec(memory_space=pl.ANY)
VMEM = pl.BlockSpec(memory_space=pltpu.VMEM)
HBM = pl.BlockSpec(memory_space=pltpu.HBM)
SMEM = pl.BlockSpec(memory_space=pltpu.SMEM)
NT = (((1,), (1,)), ((), ()))
TN = (((0,), (0,)), ((), ()))


def norm_scale(values, gain):
    return values * lax.rsqrt(jnp.mean(values * values, axis=-1, keepdims=True) + EPS) * gain


def place():
    c = lax.axis_index("ctx")
    h = lax.axis_index("fsdp")
    return h, c // 32, (c // 8) % 4, (c // 2) % 4, c % 2


def device(h, xl, z, y, core):
    return {"ctx": xl * 32 + z * 8 + y * 2 + core, "fsdp": h}


def axis_neighbour(axis, step):
    h, xl, z, y, core = place()
    if axis == "x":
        x = (2 * h + xl + step) % 4
        return device(x // 2, x % 2, z, y, core)
    if axis == "y":
        return device(h, xl, z, (y + step) % 4, core)
    return device(h, xl, (z + step) % 4, y, core)


def sibling():
    h, xl, z, y, core = place()
    return device(h, xl, z, y, 1 - core)


def greet(devices):
    barrier = pltpu.get_barrier_semaphore()
    for d in devices:
        pl.semaphore_signal(barrier, inc=1, device_id=d, device_id_type=MESH)
    pl.semaphore_wait(barrier, len(devices))


class Links:
    def __init__(self, send_sems, recv_sems):
        self.send_sems, self.recv_sems, self.count = send_sems, recv_sems, 0

    def send(self, src, dst, target):
        i = self.count
        self.count += 1
        copy = pltpu.make_async_remote_copy(
            src_ref=src,
            dst_ref=dst,
            send_sem=self.send_sems.at[i],
            recv_sem=self.recv_sems.at[i],
            device_id=target,
            device_id_type=MESH,
        )
        copy.start()
        return copy


class GatherRing:
    def __init__(self, links, axis, me, items):
        self.links, self.items = links, items
        self.me, self.left, self.right = me, (me + 3) % 4, (me + 1) % 4
        self.to_left, self.to_right = axis_neighbour(axis, 3), axis_neighbour(axis, 1)

    def start(self):
        self.first = []
        for whole, half in self.items:
            mine = whole(self.me)
            self.first.append(
                (
                    self.links.send(mine, mine, self.to_right),
                    self.links.send(mine, mine, self.to_left),
                )
            )

    def relay(self):
        self.second = []
        for (whole, half), (a, b) in zip(self.items, self.first):
            a.wait_recv()
            piece = half(self.left, 0)
            c = self.links.send(piece, piece, self.to_right)
            b.wait_recv()
            piece = half(self.right, 1)
            d = self.links.send(piece, piece, self.to_left)
            self.second.append((c, d))

    def finish(self):
        for c, d in self.second:
            c.wait_recv()
            d.wait_recv()

    def drain(self):
        for pair in self.first + self.second:
            for copy in pair:
                copy.wait_send()


def ring_of(links, axis, me, *items):
    ring = GatherRing(links, axis, me, items)
    ring.start()
    return ring


class PairGather:
    def __init__(self, links, axis, me, axis2, me2, piece, swap):
        self.links, self.axis, self.me, self.axis2, self.me2 = links, axis, me, axis2, me2
        self.piece, self.swap = piece, swap
        self.firsts, self.seconds = [], []

    def half(self, ref, k):
        return ref.at[pl.ds(64 * k, 64)]

    def spread(self, p, i):
        here = lambda j: self.piece(p, i, j)
        ring = ring_of(
            self.links, self.axis2, self.me2, (here, lambda j, k: self.half(here(j), k))
        )
        self.swap(here(self.me2))
        self.seconds.append((ring, here))

    def begin(self, p):
        here = lambda i: self.piece(p, i, self.me2)
        self.firsts.append(
            ring_of(self.links, self.axis, self.me, (here, lambda i, k: self.half(here(i), k)))
        )
        self.spread(p, self.me)

    def middle(self, p):
        ring = self.firsts[0 if len(self.seconds) == 2 else 1]
        ring.relay()
        self.spread(p, (self.me + 3) % 4)
        self.spread(p, (self.me + 1) % 4)
        ring.finish()
        self.spread(p, (self.me + 2) % 4)

    def relay(self, k):
        ring, here = self.seconds[k]
        ring.relay()
        self.swap(here((self.me2 + 3) % 4))
        self.swap(here((self.me2 + 1) % 4))

    def finish(self, k):
        ring, here = self.seconds[k]
        ring.finish()
        self.swap(here((self.me2 + 2) % 4))

    def drain(self):
        for ring in self.firsts + [ring for ring, _ in self.seconds]:
            ring.drain()


def front_kernel(
    wq, wk, wv, wo, wg, wu, wd, inputs, gain_in, gain_query, gain_key, cosine, sine,
    oq, okv, oo, og, ou, od, k_all, v_all, act_out, query_lin_out, key_lin_out, query_out,
    send_sems, recv_sems, local_sems,
):
    h, xl, z, y, core = place()
    o = 1 - h
    cross = device(1 - h, 1 - xl, z, y, core)
    other = device(h, 1 - xl, z, y, core)
    locals_ = []
    for i, (src, dst) in enumerate(
        (
            (wq, oq.at[h]),
            (wk, okv.at[h, :, pl.ds(0, 256)]),
            (wv, okv.at[h, :, pl.ds(256, 256)]),
            (wg, og.at[h]),
            (wu, ou.at[h]),
            (wd, od.at[h]),
            (wo, oo.at[h]),
        )
    ):
        copy = pltpu.make_async_copy(src, dst, local_sems.at[i])
        copy.start()
        locals_.append(copy)
    greet(
        [cross, other, sibling()]
        + [axis_neighbour(a, s) for a in ("y", "z") for s in (1, 3)]
    )
    links = Links(send_sems, recv_sems)

    def rows(i, n):
        return pl.ds(pl.multiple_of(i * n, 16), n)

    def cols(start, n):
        return pl.ds(pl.multiple_of(start, 128), n)

    def piece_g(ref, yy, zz):
        return ref.at[rows(yy, 80), cols(core * 1024 + zz * 256, 256)]

    def piece_q(ref, yy, zz):
        return ref.at[rows(yy, 80), cols(core * 512 + zz * 128, 128)]

    def piece_kv(ref, yy, zz):
        return ref.at[rows(yy, 80), cols(zz * 128, 128)]

    def piece_d(ref, yy, zz):
        return ref.at[rows((core * 4 + zz) * 4 + yy, 32)]

    def piece_o(ref, yy, zz):
        return ref.at[rows((core * 4 + yy) * 4 + zz, 16)]

    for copy in locals_[3:]:
        copy.wait()
    crosses = [
        links.send(piece(dst.at[h], y, z), piece(dst.at[h], y, z), cross)
        for dst, piece in ((og, piece_g), (od, piece_d), (ou, piece_g), (oo, piece_o))
    ]
    for copy in locals_[:3]:
        copy.wait()
    half_q = lambda ref: ref.at[:, cols(core * 512, 512)]
    half_kv = lambda ref: ref.at[:, cols(core * 256, 256)]
    directs = [
        links.send(half_kv(okv.at[h]), half_kv(okv.at[h]), cross),
        links.send(half_q(oq.at[h]), half_q(oq.at[h]), cross),
    ]
    g, u, q, d, w, kv = og.at[o], ou.at[o], oq.at[o], od.at[o], oo.at[o], okv.at[o]
    rings = []
    swaps = []

    def swap(piece):
        swaps.append(links.send(piece, piece, sibling()))

    for copy in crosses[:2]:
        copy.wait_recv()
    a1 = ring_of(
        links, "y", y,
        (
            lambda i: piece_g(g, i, z),
            lambda i, k: g.at[rows(i, 80), cols(core * 1024 + z * 256 + k * 128, 128)],
        ),
        (
            lambda i: piece_d(d, i, z),
            lambda i, k: d.at[rows(((core * 4 + z) * 4 + i) * 2 + k, 16)],
        ),
    )
    for copy in crosses[2:]:
        copy.wait_recv()
    b1 = ring_of(
        links, "z", z,
        (
            lambda i: piece_g(u, y, i),
            lambda i, k: u.at[rows(y, 80), cols(core * 1024 + i * 256 + k * 128, 128)],
        ),
        (
            lambda i: piece_o(w, y, i),
            lambda i, k: w.at[
                rows((core * 4 + y) * 4 + i, 16), pl.ds(384 * k, 256 if k else 384)
            ],
        ),
    )
    for ring in (a1, b1):
        ring.relay()
    for ring in (a1, b1):
        ring.finish()
    a2 = ring_of(
        links, "z", z,
        (
            lambda i: g.at[:, cols(core * 1024 + i * 256, 256)],
            lambda i, k: g.at[pl.ds(160 * k, 160), cols(core * 1024 + i * 256, 256)],
        ),
        (
            lambda i: d.at[rows(core * 4 + i, 128)],
            lambda i, k: d.at[rows((core * 4 + i) * 2 + k, 64)],
        ),
    )
    b2 = ring_of(
        links, "y", y,
        (
            lambda i: u.at[rows(i, 80), cols(core * 1024, 1024)],
            lambda i, k: u.at[rows(i, 80), cols(core * 1024 + k * 512, 512)],
        ),
        (
            lambda i: w.at[rows(core * 4 + i, 64)],
            lambda i, k: w.at[rows((core * 4 + i) * 2 + k, 32)],
        ),
    )
    directs[0].wait_recv()
    swap(half_kv(kv))
    a2.relay()
    b2.relay()
    directs[1].wait_recv()
    swap(half_q(q))
    swaps[0].wait_recv()

    states = inputs[...].astype(F32)
    act = norm_scale(states, gain_in[...]).astype(BF16)
    act_out[...] = act
    kv_lin = jnp.dot(act, okv[...].reshape(640, 512), preferred_element_type=F32)
    key_lin_out[...] = kv_lin[:, :256]
    cos, sin = cosine[...], sine[...]

    def turned(lin, gain):
        n = norm_scale(lin, gain)
        a, b = n[:, :128], n[:, 128:]
        return jnp.concatenate([a * cos - b * sin, b * cos + a * sin], axis=1).astype(BF16)

    k_all[xl, z, y, core] = turned(kv_lin[:, :256], gain_key[...])
    v_all[xl, z, y, core] = kv_lin[:, 256:].astype(BF16)
    own = lambda ref: ref.at[xl, z, y, core]
    first = [links.send(own(ref), own(ref), other) for ref in (k_all, v_all)]
    keys = PairGather(links, "y", y, "z", z, lambda p, i, j: k_all.at[p, j, i, core], swap)
    values = PairGather(links, "z", z, "y", y, lambda p, i, j: v_all.at[p, i, j, core], swap)
    keys.begin(xl)
    values.begin(xl)
    swaps[1].wait_recv()
    for head in range(4):
        lin = jnp.dot(
            act,
            oq[:, :, head * 256 : (head + 1) * 256].reshape(640, 256),
            preferred_element_type=F32,
        )
        query_lin_out[:, head * 256 : (head + 1) * 256] = lin
        row = turned(lin, gain_query[...])
        query_out[head * 64 : (head + 1) * 64] = row[:64]
        query_out[256 + head * 64 : 256 + (head + 1) * 64] = row[64:]

    for copy, gather in zip(first, (keys, values)):
        copy.wait_recv()
        gather.begin(1 - xl)
    for gather in (keys, values):
        gather.middle(xl)
    for gather in (keys, values):
        gather.middle(1 - xl)
    a2.finish()
    b2.finish()
    swap(g.at[:, cols(core * 1024, 1024)])
    swap(u.at[:, cols(core * 1024, 1024)])
    swap(d.at[rows(core, 512)])
    swap(w.at[rows(core, 256)])
    for k in range(8):
        for gather in (keys, values):
            gather.relay(k)
    for k in range(8):
        for gather in (keys, values):
            gather.finish(k)
    for ring in (a1, b1, a2, b2, keys, values):
        ring.drain()
    for copy in crosses + directs + first:
        copy.wait_send()
    for copy in swaps[:2]:
        copy.wait_send()
    for copy in swaps[2:]:
        copy.wait()


def front(weights, inputs, gain_in, gain_query, gain_key, cosine, sine):
    wq, wk, wv, wo, wg, wu, wd = weights
    full = lambda rows, width: jax.ShapeDtypeStruct((2, rows, width), BF16)
    kv = jax.ShapeDtypeStruct((2, 4, 4, 2, 128, 256), BF16)
    count = 6 + 32 + 2 + 4 + 2 + 2 * (2 + 8) * 4 + 2 * 8 * 4
    outs = pl.pallas_call(
        front_kernel,
        name="front",
        out_shape=(
            full(320, 1024), full(320, 512), full(512, 640), full(320, 2048), full(320, 2048),
            full(1024, 640), kv, kv,
            jax.ShapeDtypeStruct((128, 640), BF16),
            jax.ShapeDtypeStruct((128, 1024), F32),
            jax.ShapeDtypeStruct((128, 256), F32),
            jax.ShapeDtypeStruct((512, 256), BF16),
        ),
        in_specs=[HBM] * 7 + [VMEM] * 6,
        out_specs=(VMEM,) * 12,
        scratch_shapes=[
            pltpu.SemaphoreType.DMA((count,)),
            pltpu.SemaphoreType.DMA((count,)),
            pltpu.SemaphoreType.DMA((7,)),
        ],
        compiler_params=pltpu.CompilerParams(
            collective_id=1, has_side_effects=True, vmem_limit_bytes=40 << 20
        ),
    )(*weights, inputs, gain_in[None], gain_query[None], gain_key[None], cosine, sine)
    flat = [o.reshape(2 * o.shape[1], o.shape[2]) for o in outs[:6]]
    return flat + [o.reshape(64, 128, 256) for o in outs[6:8]] + list(outs[8:])


def add_into(dst, src, lead):
    if not lead:
        dst[...] = (dst[...].astype(F32) + src[...].astype(F32)).astype(dst.dtype)
        return

    @pl.loop(0, lead[0])
    def _(i):
        add_into(dst.at[i], src.at[i], lead[1:])


def sum_into(dst, terms, lead):
    if not lead:
        total = terms[0][...].astype(F32)
        for t in terms[1:]:
            total = total + t[...].astype(F32)
        dst[...] = total.astype(dst.dtype)
        return

    @pl.loop(0, lead[0])
    def _(i):
        sum_into(dst.at[i], [t.at[i] for t in terms], lead[1:])


class SumRing:
    def __init__(self, links, axis, me, block, half, pass0, pass1, from_left, from_right, part, lead, half_lead):
        self.links = links
        self.me, self.left, self.right, self.far = me, (me + 3) % 4, (me + 1) % 4, (me + 2) % 4
        self.to_left, self.to_right = axis_neighbour(axis, 3), axis_neighbour(axis, 1)
        self.block, self.half = block, half
        self.pass0, self.pass1 = pass0, pass1
        self.from_left, self.from_right = from_left, from_right
        self.part, self.lead, self.half_lead = part, lead, half_lead

    def start(self, ready):
        send = self.links.send
        ready(self.far)
        self.a = send(self.half(self.far, 0), self.pass0, self.to_right)
        self.b = send(self.half(self.far, 1), self.pass1, self.to_left)
        ready(self.right)
        self.c = send(self.half(self.right, 1), self.part(self.from_left, 1), self.to_right)
        ready(self.left)
        self.d = send(self.half(self.left, 0), self.part(self.from_right, 0), self.to_left)
        ready(self.me)

    def relay(self):
        send = self.links.send
        self.a.wait_recv()
        add_into(self.half(self.right, 0), self.pass0, self.half_lead)
        self.e = send(self.half(self.right, 0), self.part(self.from_left, 0), self.to_right)
        self.b.wait_recv()
        add_into(self.half(self.left, 1), self.pass1, self.half_lead)
        self.f = send(self.half(self.left, 1), self.part(self.from_right, 1), self.to_left)

    def finish(self, out):
        for copy in (self.c, self.d, self.e, self.f):
            copy.wait_recv()
        sum_into(out, [self.block(self.me), self.from_left, self.from_right], self.lead)

    def drain(self):
        for copy in (self.a, self.b, self.c, self.d, self.e, self.f):
            copy.wait_send()


class Direct:
    def __init__(self, links, axis, me, block, got):
        self.links, self.axis, self.me, self.block, self.got = links, axis, me, block, got

    def start(self):
        self.copies = [
            self.links.send(
                self.block((self.me + step) % 4), self.got.at[step - 1], axis_neighbour(self.axis, step)
            )
            for step in (1, 2, 3)
        ]

    def finish(self, out):
        for copy in self.copies:
            copy.wait_recv()
        sum_into(out, [self.block(self.me)] + [self.got.at[i] for i in range(3)], ())

    def drain(self):
        for copy in self.copies:
            copy.wait_send()


def nothing(i):
    pass


def first_half(ref, k):
    return ref.at[pl.ds(2 * k, 2)]


class KeySum:
    SCRATCH = 12

    def __init__(self, links, source, out, scratch, axes):
        h, xl, z, y, core = place()
        self.links, self.source, self.out, self.axes = links, source, out, axes
        self.xl, self.core, self.me = xl, core, {"y": y, "z": z}
        self.got, self.p0, self.p1, self.fl, self.fr, self.second, self.q0, self.q1, self.gl, self.gr, self.third, self.last = scratch
        self.other = device(h, 1 - xl, z, y, core)

    @staticmethod
    def scratch():
        buf = lambda *lead: pltpu.VMEM(lead + (128, 256), BF16)
        return [buf(2, 4, 4), buf(4), buf(4), buf(2, 4), buf(2, 4), buf(2, 4), buf(), buf(), buf(2), buf(2), buf(2), buf()]

    def at(self, ref, i, *more):
        return ref.at[(slice(None), i, slice(None)) + more] if self.axes[0] == "z" else ref.at[(slice(None), slice(None), i) + more]

    def swap(self):
        me = self.me[self.axes[0]]
        self.swaps = [
            self.links.send(self.at(self.source, i, 1 - self.core), self.at(self.got, i), sibling())
            for i in ((me + 2) % 4, (me + 1) % 4, (me + 3) % 4, me)
        ]
        self.pending = list(self.swaps)

    def ready(self, i):
        self.pending.pop(0).wait_recv()
        mine, got = self.at(self.source, i, self.core), self.at(self.got, i)
        add_into(got, mine, (2, 4))

    def start(self):
        first, second = self.axes
        half = lambda i, k: self.got.at[(k, i) if first == "z" else (k, slice(None), i)]
        self.ring = SumRing(
            self.links, first, self.me[first], lambda i: self.at(self.got, i), half,
            self.p0, self.p1, self.fl, self.fr, lambda ref, k: ref.at[k], (2, 4), (4,),
        )
        self.ring2 = SumRing(
            self.links, second, self.me[second], lambda i: self.second.at[:, i],
            lambda i, k: self.second.at[k, i],
            self.q0, self.q1, self.gl, self.gr, lambda ref, k: ref.at[k], (2,), (),
        )
        self.ring.start(self.ready)

    def relay(self):
        self.ring.relay()

    def next(self):
        self.ring.finish(self.second)
        self.ring2.start(nothing)

    def relay2(self):
        self.ring2.relay()

    def next2(self):
        self.ring2.finish(self.third)
        self.copy = self.links.send(self.third.at[1 - self.xl], self.last, self.other)

    def finish(self):
        self.copy.wait_recv()
        sum_into(self.out, [self.third.at[self.xl], self.last], ())

    def drain(self):
        self.ring.drain()
        self.ring2.drain()
        for copy in self.swaps + [self.copy]:
            copy.wait_send()


class WeightSum:
    SCRATCH = 14

    def __init__(self, links, source, out, scratch, axes, local_sem):
        h, xl, z, y, core = place()
        self.links, self.source, self.out, self.axes = links, source, out, axes
        self.core, self.me = core, {"x": 2 * h + xl, "y": y, "z": z}
        (
            self.own, self.got, self.total, self.p0, self.p1, self.fl, self.fr,
            self.total2, self.q0, self.q1, self.gl, self.gr, self.total3, self.last,
        ) = scratch
        self.local = pltpu.make_async_copy(source.at[:, :, :, core], self.own, local_sem)
        self.local.start()

    @staticmethod
    def scratch(rows):
        buf = lambda *lead: pltpu.VMEM(lead + (rows, 128), BF16)
        return (
            [buf(2, 4, 4, 2)] * 2
            + [buf(4, 4, 4), buf(2, 4), buf(2, 4), buf(4, 4), buf(4, 4)]
            + [buf(4, 4), buf(2), buf(2), buf(4), buf(4), buf(4), buf(3)]
        )

    def at(self, ref, i, core=None):
        every = slice(None)
        mid = () if core is None else (core,)
        spot = {
            "x": (i % 2, every, every) + mid + (i // 2,),
            "y": (every, every, i) + mid,
            "z": (every, i, every) + mid,
        }[self.axes[0]]
        return ref.at[spot]

    def swap(self):
        me = self.me[self.axes[0]]
        self.swaps = [
            self.links.send(self.at(self.source, i, 1 - self.core), self.at(self.got, i), sibling())
            for i in ((me + 2) % 4, (me + 1) % 4, (me + 3) % 4, me)
        ]
        self.pending = list(self.swaps)

    def ready(self, i):
        self.pending.pop(0).wait_recv()

        @pl.loop(0, 4)
        def _(j):
            @pl.loop(0, 4)
            def _(k):
                spot = dict(zip(self.axes, (i, j, k)))
                x, y, z = spot["x"], spot["y"], spot["z"]
                where = (x % 2, z, y, x // 2)
                sum_into(self.total.at[i, j, k], [self.own.at[where], self.got.at[where]], ())

    def start(self):
        first, second, third = self.axes
        self.local.wait()
        self.ring = SumRing(
            self.links, first, self.me[first], lambda i: self.total.at[i],
            lambda i, k: first_half(self.total.at[i], k),
            self.p0, self.p1, self.fl, self.fr, first_half, (4, 4), (2, 4),
        )
        self.ring2 = SumRing(
            self.links, second, self.me[second], lambda i: self.total2.at[i],
            lambda i, k: first_half(self.total2.at[i], k),
            self.q0, self.q1, self.gl, self.gr, first_half, (4,), (2,),
        )
        self.direct = Direct(
            self.links, third, self.me[third], lambda i: self.total3.at[i], self.last
        )
        self.ring.start(self.ready)

    def relay(self):
        self.ring.relay()

    def next(self):
        self.ring.finish(self.total2)
        self.ring2.start(nothing)

    def relay2(self):
        self.ring2.relay()

    def next2(self):
        self.ring2.finish(self.total3)
        self.direct.start()

    def finish(self):
        self.direct.finish(self.out)

    def drain(self):
        self.ring.drain()
        self.ring2.drain()
        self.direct.drain()
        for copy in self.swaps:
            copy.wait_send()


def sum_kernel(orders, n_kv, *refs):
    n = n_kv + len(orders)
    sources, outs, rest = refs[:n], refs[n : 2 * n], list(refs[2 * n :])
    send_sems, recv_sems, local_sems = rest[-3:]
    h, xl, z, y, core = place()
    greet(
        [sibling()] + [axis_neighbour(a, s) for a in ("x", "y", "z") for s in (1, 2, 3)]
    )
    links = Links(send_sems, recv_sems)
    sums = []
    for t in range(n):
        if t < n_kv:
            scratch, rest = rest[: KeySum.SCRATCH], rest[KeySum.SCRATCH :]
            sums.append(KeySum(links, sources[t], outs[t], scratch, ("zy", "yz")[t]))
        else:
            scratch, rest = rest[: WeightSum.SCRATCH], rest[WeightSum.SCRATCH :]
            sums.append(
                WeightSum(
                    links, sources[t], outs[t], scratch, orders[t - n_kv], local_sems.at[t]
                )
            )
    for stage in ("swap", "start", "relay", "next", "relay2", "next2", "finish", "drain"):
        for s in sums:
            getattr(s, stage)()


def sum_up(name, collective_id, grads, orders, kv=()):
    scratch, outs, count = [], [], 0
    for _ in kv:
        scratch += KeySum.scratch()
        outs.append(jax.ShapeDtypeStruct((128, 256), F32))
        count += 4 + 12 + 1
    for g in grads:
        scratch += WeightSum.scratch(g.shape[1])
        outs.append(jax.ShapeDtypeStruct(g.shape[1:], F32))
        count += 4 + 12 + 3
    n = len(outs)
    return pl.pallas_call(
        functools.partial(sum_kernel, orders, len(kv)),
        name=name,
        out_shape=tuple(outs),
        in_specs=[VMEM] * len(kv) + [HBM] * len(grads),
        out_specs=(VMEM,) * n,
        scratch_shapes=scratch
        + [
            pltpu.SemaphoreType.DMA((count,)),
            pltpu.SemaphoreType.DMA((count,)),
            pltpu.SemaphoreType.DMA((n,)),
        ],
        compiler_params=pltpu.CompilerParams(
            collective_id=collective_id, has_side_effects=True, vmem_limit_bytes=40 << 20
        ),
    )(
        *[g.reshape((2, 4, 4, 2) + g.shape[1:]) for g in kv],
        *[g.reshape((2, 4, 4, 2, 2) + g.shape[1:]) for g in grads],
    )


def tile(ref, inverse, step):
    parts = []
    for j in range(8):
        block = step * 8 + j
        late = block >= 64
        owner = inverse[jnp.where(late, 127 - block, block)]
        half = pl.multiple_of(jnp.where(late, 64, 0), 64)
        parts.append(ref[owner, pl.ds(half, 64), :])
    return jnp.concatenate(parts, axis=0)


def attention_kernel(inverse, pair, query, keys, values, out, sums, acc, weight):
    own = pair[0]

    def rows_of(part):
        return pl.ds(part * 256, 256)

    acc[...] = jnp.zeros_like(acc)
    weight[...] = jnp.zeros_like(weight)

    def step_for(part, block, step, masked):
        k = tile(keys, inverse, step)
        v = tile(values, inverse, step)
        q = query[rows_of(part), :]
        raw = lax.dot_general(q, k, NT, preferred_element_type=F32)
        p = jnp.exp2(raw * EXP2_SCALE)
        if masked:
            token = lax.broadcasted_iota(jnp.int32, (256, 512), 0) % 64 + block * 64
            position = lax.broadcasted_iota(jnp.int32, (256, 512), 1) + step * 512
            p = jnp.where(position <= token, p, 0.0)
        w = p[:, :128] + p[:, 128:256] + p[:, 256:384] + p[:, 384:]
        weight[rows_of(part), :] += w
        acc[rows_of(part), :] += jnp.dot(p.astype(BF16), v, preferred_element_type=F32)

    for part in range(2):
        block = own if part == 0 else 127 - own
        full = block // 8

        @pl.loop(0, full)
        def _(step):
            step_for(part, block, step, False)

        step_for(part, block, full, True)
    total = jnp.sum(weight[...], axis=1, keepdims=True)
    out[...] = acc[...] / total
    sums[...] = total


def attention(inverse, pair, query, keys, values):
    return pl.pallas_call(
        attention_kernel,
        name="attention_forward",
        out_shape=(
            jax.ShapeDtypeStruct((512, 256), F32),
            jax.ShapeDtypeStruct((512, 1), F32),
        ),
        in_specs=[SMEM, SMEM, VMEM, VMEM, VMEM],
        out_specs=(VMEM, VMEM),
        scratch_shapes=[pltpu.VMEM((512, 256), F32), pltpu.VMEM((512, 128), F32)],
        compiler_params=pltpu.CompilerParams(vmem_limit_bytes=10 << 20),
    )(inverse, pair, query, keys, values)


def attention_back_kernel(
    inverse, pair, query, d_out, log_sum, delta, keys, values, d_query, d_keys, d_values
):
    own = pair[0]
    d_query[...] = jnp.zeros_like(d_query)

    def terms(part, step, k, v, masked):
        rows = pl.ds(part * 256, 256)
        block = own if part == 0 else 127 - own
        q = query[rows, :]
        g = d_out[rows, :]
        raw = lax.dot_general(k, q, NT, preferred_element_type=F32)
        p = jnp.exp2(raw * EXP2_SCALE - log_sum[:, rows])
        if masked:
            position = lax.broadcasted_iota(jnp.int32, (512, 256), 0) + step * 512
            token = lax.broadcasted_iota(jnp.int32, (512, 256), 1) % 64 + block * 64
            p = jnp.where(position <= token, p, 0.0)
        d_p = lax.dot_general(v, g, NT, preferred_element_type=F32)
        d_s = (p * (d_p - delta[:, rows])).astype(BF16)
        d_query[rows, :] += lax.dot_general(d_s, k, TN, preferred_element_type=F32)
        d_k = jnp.dot(d_s, q, preferred_element_type=F32)
        d_v = jnp.dot(p.astype(BF16), g, preferred_element_type=F32)
        return d_k, d_v

    def store(step, d_k, d_v):
        for j in range(8):
            block = step * 8 + j
            late = block >= 64
            owner = inverse[jnp.where(late, 127 - block, block)]
            half = pl.multiple_of(jnp.where(late, 64, 0), 64)
            d_keys[owner, pl.ds(half, 64), :] = (d_k[j * 64 : (j + 1) * 64] * SCALE).astype(BF16)
            d_values[owner, pl.ds(half, 64), :] = d_v[j * 64 : (j + 1) * 64].astype(BF16)

    early_full = own // 8
    late_full = (127 - own) // 8

    @pl.loop(0, early_full)
    def _(step):
        k = tile(keys, inverse, step)
        v = tile(values, inverse, step)
        d_k, d_v = terms(1, step, k, v, False)
        d_k2, d_v2 = terms(0, step, k, v, False)
        store(step, d_k + d_k2, d_v + d_v2)

    k = tile(keys, inverse, early_full)
    v = tile(values, inverse, early_full)
    d_k, d_v = terms(1, early_full, k, v, False)
    d_k2, d_v2 = terms(0, early_full, k, v, True)
    store(early_full, d_k + d_k2, d_v + d_v2)

    @pl.loop(early_full + 1, late_full)
    def _(step):
        d_k, d_v = terms(1, step, tile(keys, inverse, step), tile(values, inverse, step), False)
        store(step, d_k, d_v)

    d_k, d_v = terms(
        1, late_full, tile(keys, inverse, late_full), tile(values, inverse, late_full), True
    )
    store(late_full, d_k, d_v)
    zero = jnp.zeros((512, 256), F32)

    @pl.loop(late_full + 1, 16)
    def _(step):
        store(step, zero, zero)

    d_query[...] = d_query[...] * SCALE


def attention_back(inverse, pair, query, d_out, log_sum, delta, keys, values):
    return pl.pallas_call(
        attention_back_kernel,
        name="attention_backward",
        out_shape=(
            jax.ShapeDtypeStruct((512, 256), F32),
            jax.ShapeDtypeStruct(keys.shape, BF16),
            jax.ShapeDtypeStruct(keys.shape, BF16),
        ),
        in_specs=[SMEM, SMEM] + [VMEM] * 6,
        out_specs=(VMEM,) * 3,
        compiler_params=pltpu.CompilerParams(vmem_limit_bytes=10 << 20),
    )(inverse, pair, query, d_out, log_sum, delta, keys, values)


def rotate(values, angles):
    half = values.shape[-1] // 2
    first = values[..., :half]
    second = values[..., half:]
    cosine = jnp.cos(angles)
    sine = jnp.sin(angles)
    return jnp.concatenate(
        [first * cosine - second * sine, second * cosine + first * sine], axis=-1
    )


def head_rows(values):
    return values.reshape(2, 64, 4, 256).transpose(0, 2, 1, 3).reshape(512, 256)


def token_rows(values):
    return values.reshape(2, 4, 64, 256).transpose(0, 2, 1, 3).reshape(128, 1024)


def local(
    inputs,
    pair_order,
    w_query,
    w_key,
    w_value,
    w_output,
    w_gate,
    w_up,
    w_down,
    gain_in,
    gain_query,
    gain_key,
    gain_post_attn,
    gain_pre_ff,
    gain_post_ff,
    cotangent,
):
    f32, bf16 = F32, BF16
    rows = 128
    me_index = lax.axis_index("ctx")
    own_pair = lax.dynamic_slice_in_dim(pair_order, me_index, 1)
    within = jnp.arange(rows, dtype=jnp.int32)
    block_id = jnp.where(within < 64, own_pair, 127 - own_pair)
    positions = block_id * 64 + within % 64
    freq = ROPE_BASE ** (-jnp.arange(128, dtype=f32) / 128)
    angles = positions.astype(f32)[:, None] * freq
    matches = pair_order[None, :] == jnp.arange(64, dtype=jnp.int32)[:, None]
    inverse = jnp.sum(jnp.where(matches, jnp.arange(64, dtype=jnp.int32)[None, :], 0), axis=1)

    def prepare(query_lin, key_lin, g_query, g_key):
        query = rotate(
            norm_scale(query_lin.reshape(rows, 4, 256), g_query), angles[:, None, :]
        )
        key = rotate(norm_scale(key_lin, g_key), angles)
        return (query, key)

    states = inputs[0].astype(f32)
    (
        wq_all, wkv_all, wo_all, wg_all, wu_all, wd_all, k_all, v_all,
        act_one, query_lin, key_lin, query_b,
    ) = front(
        (w_query, w_key, w_value, w_output, w_gate, w_up, w_down),
        inputs[0], gain_in, gain_query, gain_key, jnp.cos(angles), jnp.sin(angles),
    )
    attended, weight_sum = attention(inverse, own_pair, query_b, k_all, v_all)
    attended_flat = token_rows(attended.astype(bf16))
    att_lin = jnp.dot(attended_flat, wo_all, preferred_element_type=f32)
    resid = states + norm_scale(att_lin, gain_post_attn)
    act_two = norm_scale(resid, gain_pre_ff).astype(bf16)
    gate = jnp.dot(act_two, wg_all, preferred_element_type=f32)
    upper = jnp.dot(act_two, wu_all, preferred_element_type=f32)
    hidden_b = (jax.nn.gelu(gate, approximate=True) * upper).astype(bf16)
    down = jnp.dot(hidden_b, wd_all, preferred_element_type=f32)
    layer_out = resid + norm_scale(down, gain_post_ff)
    grad_y = cotangent[0].astype(f32)
    unused_out, post_ff_back = jax.vjp(norm_scale, down, gain_post_ff)
    d_down, d_gain_post_ff = post_ff_back(grad_y)
    d_down_b = d_down.astype(bf16)
    grad_down = jnp.einsum("rf,rd->fd", hidden_b, d_down_b, preferred_element_type=f32)
    d_hidden = jnp.einsum("rd,fd->rf", d_down_b, wd_all, preferred_element_type=f32)
    unused_act, act_back = jax.vjp(
        lambda gate_in, up_in: jax.nn.gelu(gate_in, approximate=True) * up_in, gate, upper
    )
    d_gate, d_upper = act_back(d_hidden)
    d_gate_b = d_gate.astype(bf16)
    d_upper_b = d_upper.astype(bf16)
    grad_gate = jnp.einsum("rd,rf->df", act_two, d_gate_b, preferred_element_type=f32)
    grad_up = jnp.einsum("rd,rf->df", act_two, d_upper_b, preferred_element_type=f32)
    d_act_two = jnp.einsum("rf,df->rd", d_gate_b, wg_all, preferred_element_type=f32) + jnp.einsum(
        "rf,df->rd", d_upper_b, wu_all, preferred_element_type=f32
    )
    unused_two, pre_ff_back = jax.vjp(norm_scale, resid, gain_pre_ff)
    d_resid_part, d_gain_pre_ff = pre_ff_back(d_act_two)
    grad_resid = grad_y + d_resid_part
    unused_three, post_attn_back = jax.vjp(norm_scale, att_lin, gain_post_attn)
    d_att, d_gain_post_attn = post_attn_back(grad_resid)
    d_att_b = d_att.astype(bf16)
    grad_output = jnp.einsum("re,rd->ed", attended_flat, d_att_b, preferred_element_type=f32)
    d_attended_b = head_rows(
        jnp.einsum("rd,ed->re", d_att_b, wo_all, preferred_element_type=f32).astype(bf16)
    )
    row_delta = jnp.sum(d_attended_b.astype(f32) * attended, axis=1)
    d_query_rows, d_keys, d_values = attention_back(
        inverse,
        own_pair,
        query_b,
        d_attended_b,
        jnp.log2(weight_sum).reshape(1, 512),
        row_delta[None, :],
        k_all,
        v_all,
    )
    split = lambda g: g.astype(bf16).reshape(128, -1, 128)
    d_key_own, d_value_own, s_down, s_gate, s_up, s_output = sum_up(
        "sum_first",
        3,
        [split(grad_down), split(grad_gate), split(grad_up), split(grad_output)],
        ("xyz", "xzy", "yzx", "zxy"),
        (d_keys, d_values),
    )
    d_value_b = d_value_own.astype(bf16)
    d_query = token_rows(d_query_rows).reshape(rows, 4, 256)
    unused_four, prep_back = jax.vjp(prepare, query_lin, key_lin, gain_query, gain_key)
    d_query_lin, d_key_lin, d_gain_query, d_gain_key = prep_back((d_query, d_key_own))
    d_query_lin_b = d_query_lin.astype(bf16).reshape(rows, 1024)
    d_kv_lin_b = jnp.concatenate([d_key_lin.astype(bf16), d_value_b], axis=1)
    grad_query = jnp.einsum("rd,re->de", act_one, d_query_lin_b, preferred_element_type=f32)
    grad_kv = jnp.einsum("rd,re->de", act_one, d_kv_lin_b, preferred_element_type=f32)
    d_act_one = jnp.einsum("re,de->rd", d_query_lin_b, wq_all, preferred_element_type=f32)
    d_act_one = d_act_one + jnp.einsum("re,de->rd", d_kv_lin_b, wkv_all, preferred_element_type=f32)
    unused_five, pre_attn_back = jax.vjp(norm_scale, states, gain_in)
    d_states, d_gain_in = pre_attn_back(d_act_one)
    input_grad = grad_resid + d_states

    gains = jnp.concatenate(
        [
            g.reshape(128, -1)
            for g in (
                d_gain_in,
                d_gain_post_attn,
                d_gain_pre_ff,
                d_gain_post_ff,
                d_gain_query,
                d_gain_key,
            )
        ],
        axis=1,
    )
    gains = jnp.pad(gains, ((0, 0), (0, 128 - gains.shape[1]))).astype(bf16)[:, None, :]
    tail = jnp.concatenate([split(grad_kv), gains, jnp.zeros((128, 11, 128), bf16)], axis=1)
    s_query, s_tail = sum_up("sum_last", 4, [split(grad_query), tail], ("xyz", "yzx"))
    s_down = s_down.reshape(16, 640)
    s_gate = s_gate.reshape(5, 2048)
    s_up = s_up.reshape(5, 2048)
    s_output = s_output.reshape(8, 640)
    s_query = s_query.reshape(5, 1024)
    s_kv = s_tail[:20].reshape(5, 512)
    s_gains = s_tail[20]
    return (
        layer_out.astype(bf16)[None],
        input_grad.astype(bf16)[None],
        s_query,
        s_kv[:, :256],
        s_kv[:, 256:],
        s_output,
        s_gate,
        s_up,
        s_down,
        s_gains[0:5],
        s_gains[20:22],
        s_gains[22:24],
        s_gains[5:10],
        s_gains[10:15],
        s_gains[15:20],
    )


def solution(mesh):
    placed = (
        P("fsdp", "ctx", None),
        P(),
        P("fsdp", None),
        P("fsdp", None),
        P("fsdp", None),
        P("fsdp", None),
        P("fsdp", None),
        P("fsdp", None),
        P("fsdp", None),
        P(),
        P(),
        P(),
        P(),
        P(),
        P(),
        P("fsdp", "ctx", None),
    )
    both = ("ctx", "fsdp")
    return jax.shard_map(
        local,
        mesh=mesh,
        in_specs=placed,
        out_specs=(P("fsdp", "ctx", None),) * 2 + (P(both, None),) * 7 + (P(both),) * 6,
        check_vma=False,
    )
```

```python
import functools
import math

import jax
import jax.numpy as jnp
from jax import lax
from jax.experimental import pallas as pl
from jax.experimental.pallas import tpu as pltpu
from jax.sharding import PartitionSpec as P

EPS = 1e-06
ROPE_BASE = 1000000.0
SCALE = 0.0625
EXP2_SCALE = SCALE * math.log2(math.e)
MESH = pl.DeviceIdType.MESH
BF16 = jnp.bfloat16
F32 = jnp.float32
ANY = pl.BlockSpec(memory_space=pl.ANY)
VMEM = pl.BlockSpec(memory_space=pltpu.VMEM)
HBM = pl.BlockSpec(memory_space=pltpu.HBM)
SMEM = pl.BlockSpec(memory_space=pltpu.SMEM)
NT = (((1,), (1,)), ((), ()))
TN = (((0,), (0,)), ((), ()))


def norm_scale(values, gain):
    return values * lax.rsqrt(jnp.mean(values * values, axis=-1, keepdims=True) + EPS) * gain


def place():
    c = lax.axis_index("ctx")
    h = lax.axis_index("fsdp")
    return h, c // 32, (c // 8) % 4, (c // 2) % 4, c % 2


def device(h, xl, z, y, core):
    return {"ctx": xl * 32 + z * 8 + y * 2 + core, "fsdp": h}


def axis_neighbour(axis, step):
    h, xl, z, y, core = place()
    if axis == "x":
        x = (2 * h + xl + step) % 4
        return device(x // 2, x % 2, z, y, core)
    if axis == "y":
        return device(h, xl, z, (y + step) % 4, core)
    return device(h, xl, (z + step) % 4, y, core)


def sibling():
    h, xl, z, y, core = place()
    return device(h, xl, z, y, 1 - core)


def greet(devices):
    barrier = pltpu.get_barrier_semaphore()
    for d in devices:
        pl.semaphore_signal(barrier, inc=1, device_id=d, device_id_type=MESH)
    pl.semaphore_wait(barrier, len(devices))


class Links:
    def __init__(self, send_sems, recv_sems):
        self.send_sems, self.recv_sems, self.count = send_sems, recv_sems, 0

    def send(self, src, dst, target):
        i = self.count
        self.count += 1
        assert i < self.send_sems.shape[0]
        copy = pltpu.make_async_remote_copy(
            src_ref=src,
            dst_ref=dst,
            send_sem=self.send_sems.at[i],
            recv_sem=self.recv_sems.at[i],
            device_id=target,
            device_id_type=MESH,
        )
        copy.start()
        return copy


class GatherRing:
    def __init__(self, links, axis, me, items):
        self.links, self.items = links, items
        self.me, self.left, self.right = me, (me + 3) % 4, (me + 1) % 4
        self.to_left, self.to_right = axis_neighbour(axis, 3), axis_neighbour(axis, 1)

    def start(self):
        self.first = []
        for whole, half in self.items:
            mine = whole(self.me)
            self.first.append(
                (
                    self.links.send(mine, mine, self.to_right),
                    self.links.send(mine, mine, self.to_left),
                )
            )

    def relay(self):
        self.second = []
        for (whole, half), (a, b) in zip(self.items, self.first):
            a.wait_recv()
            piece = half(self.left, 0)
            c = self.links.send(piece, piece, self.to_right)
            b.wait_recv()
            piece = half(self.right, 1)
            d = self.links.send(piece, piece, self.to_left)
            self.second.append((c, d))

    def finish(self):
        for c, d in self.second:
            c.wait_recv()
            d.wait_recv()

    def drain(self):
        for pair in self.first + self.second:
            for copy in pair:
                copy.wait_send()


def ring_of(links, axis, me, *items):
    ring = GatherRing(links, axis, me, items)
    ring.start()
    return ring


class PairGather:
    def __init__(self, links, axis, me, axis2, me2, piece, swap):
        self.links, self.axis, self.me, self.axis2, self.me2 = links, axis, me, axis2, me2
        self.piece, self.swap = piece, swap
        self.firsts, self.seconds = [], []

    def half(self, ref, k):
        return ref.at[pl.ds(64 * k, 64)]

    def spread(self, p, i):
        here = lambda j: self.piece(p, i, j)
        ring = ring_of(
            self.links, self.axis2, self.me2, (here, lambda j, k: self.half(here(j), k))
        )
        self.swap(here(self.me2))
        self.seconds.append((ring, here))

    def begin(self, p):
        here = lambda i: self.piece(p, i, self.me2)
        self.firsts.append(
            ring_of(self.links, self.axis, self.me, (here, lambda i, k: self.half(here(i), k)))
        )
        self.spread(p, self.me)

    def middle(self, p):
        ring = self.firsts[0 if len(self.seconds) == 2 else 1]
        ring.relay()
        self.spread(p, (self.me + 3) % 4)
        self.spread(p, (self.me + 1) % 4)
        ring.finish()
        self.spread(p, (self.me + 2) % 4)

    def relay(self, k):
        ring, here = self.seconds[k]
        ring.relay()
        self.swap(here((self.me2 + 3) % 4))
        self.swap(here((self.me2 + 1) % 4))

    def finish(self, k):
        ring, here = self.seconds[k]
        ring.finish()
        self.swap(here((self.me2 + 2) % 4))

    def drain(self):
        for ring in self.firsts + [ring for ring, _ in self.seconds]:
            ring.drain()


def front_kernel(
    wq, wk, wv, wo, wg, wu, wd, inputs, gains, cosine, sine,
    oq, okv, oo, og, ou, od, k_all, v_all, act_out, query_lin_out, key_lin_out, query_out,
    send_sems, recv_sems, local_sems,
):
    h, xl, z, y, core = place()
    o = 1 - h
    cross = device(1 - h, 1 - xl, z, y, core)
    other = device(h, 1 - xl, z, y, core)
    locals_ = []
    for i, (src, dst) in enumerate(
        (
            (wq, oq.at[h]),
            (wk, okv.at[h, :, pl.ds(0, 256)]),
            (wv, okv.at[h, :, pl.ds(256, 256)]),
            (wg, og.at[h]),
            (wu, ou.at[h]),
            (wd, od.at[h]),
            (wo, oo.at[h]),
        )
    ):
        copy = pltpu.make_async_copy(src, dst, local_sems.at[i])
        copy.start()
        locals_.append(copy)
    greet(
        [cross, other, sibling()]
        + [axis_neighbour(a, s) for a in ("y", "z") for s in (1, 3)]
    )
    links = Links(send_sems, recv_sems)

    def rows(i, n):
        return pl.ds(pl.multiple_of(i * n, 16), n)

    def cols(start, n):
        return pl.ds(pl.multiple_of(start, 128), n)

    def piece_g(ref, yy, zz):
        return ref.at[rows(yy, 80), cols(core * 1024 + zz * 256, 256)]

    def piece_kv(ref, yy, zz):
        return ref.at[rows(yy, 80), cols(zz * 128, 128)]

    def piece_o(ref, yy, zz):
        return ref.at[rows((core * 4 + zz) * 4 + yy, 16)]

    for copy in locals_[:3]:
        copy.wait()
    crosses = [links.send(piece_kv(okv.at[h], y, z), piece_kv(okv.at[h], y, z), cross)]
    for copy in locals_[3:]:
        copy.wait()
    crosses += [
        links.send(piece(dst.at[h], y, z), piece(dst.at[h], y, z), cross)
        for dst, piece in ((og, piece_g), (oo, piece_o), (ou, piece_g))
    ]
    half_q = lambda ref: ref.at[:, cols(core * 512, 512)]
    half_d = lambda ref: ref.at[rows(core, 512)]
    direct_q = links.send(half_q(oq.at[h]), half_q(oq.at[h]), cross)
    g, u, q, d, w, kv = og.at[o], ou.at[o], oq.at[o], od.at[o], oo.at[o], okv.at[o]
    swaps = []

    def swap(piece):
        swaps.append(links.send(piece, piece, sibling()))

    crosses[0].wait_recv()
    kv1 = ring_of(
        links, "z", z,
        (
            lambda i: piece_kv(kv, y, i),
            lambda i, k: kv.at[
                pl.ds(pl.multiple_of(y * 80 + k * 48, 16), 32 if k else 48), cols(i * 128, 128)
            ],
        ),
    )
    for copy in crosses[1:3]:
        copy.wait_recv()
    a1 = ring_of(
        links, "y", y,
        (
            lambda i: piece_g(g, i, z),
            lambda i, k: g.at[rows(i, 80), cols(core * 1024 + z * 256 + k * 128, 128)],
        ),
        (
            lambda i: piece_o(w, i, z),
            lambda i, k: w.at[
                rows((core * 4 + z) * 4 + i, 16), pl.ds(384 * k, 256 if k else 384)
            ],
        ),
    )
    crosses[3].wait_recv()
    b1 = ring_of(
        links, "z", z,
        (
            lambda i: piece_g(u, y, i),
            lambda i, k: u.at[rows(y, 80), cols(core * 1024 + i * 256 + k * 128, 128)],
        ),
    )
    kv1.relay()
    a1.relay()
    b1.relay()
    kv1.finish()
    kv2 = ring_of(
        links, "y", y,
        (lambda i: kv.at[rows(i, 80)], lambda i, k: kv.at[rows(i, 80), pl.ds(256 * k, 256)]),
    )
    a1.finish()
    a2 = ring_of(
        links, "z", z,
        (
            lambda i: g.at[:, cols(core * 1024 + i * 256, 256)],
            lambda i, k: g.at[pl.ds(160 * k, 160), cols(core * 1024 + i * 256, 256)],
        ),
        (
            lambda i: w.at[rows(core * 4 + i, 64)],
            lambda i, k: w.at[rows((core * 4 + i) * 2 + k, 32)],
        ),
    )
    b1.finish()
    kv2.relay()
    b2 = ring_of(
        links, "y", y,
        (
            lambda i: u.at[rows(i, 80), cols(core * 1024, 1024)],
            lambda i, k: u.at[rows(i, 80), cols(core * 1024 + k * 512, 512)],
        ),
    )
    kv2.finish()

    states = inputs[...].astype(F32)
    act = norm_scale(states, gains[0:1]).astype(BF16)
    act_out[...] = act
    kv_lin = jnp.dot(act, okv[...].reshape(640, 512), preferred_element_type=F32)
    key_lin_out[...] = kv_lin[:, :256]
    cos, sin = cosine[...], sine[...]

    def turned(lin, gain):
        n = norm_scale(lin, gain)
        a, b = n[:, :128], n[:, 128:]
        return jnp.concatenate([a * cos - b * sin, b * cos + a * sin], axis=1).astype(BF16)

    k_all[xl, z, y, core] = turned(kv_lin[:, :256], gains[2:3, :256])
    v_all[xl, z, y, core] = kv_lin[:, 256:].astype(BF16)
    own = lambda ref: ref.at[xl, z, y, core]
    first = [links.send(own(ref), own(ref), other) for ref in (k_all, v_all)]
    keys = PairGather(links, "y", y, "z", z, lambda p, i, j: k_all.at[p, j, i, core], swap)
    values = PairGather(links, "z", z, "y", y, lambda p, i, j: v_all.at[p, i, j, core], swap)
    keys.begin(xl)
    values.begin(xl)
    direct_q.wait_recv()
    swap(half_q(q))
    swap_q = swaps.pop()
    direct_d = links.send(half_d(od.at[h]), half_d(od.at[h]), cross)
    a2.relay()
    b2.relay()
    for copy, gather in zip(first, (keys, values)):
        copy.wait_recv()
        gather.begin(1 - xl)
    swap_q.wait_recv()
    for head in range(4):
        lin = jnp.dot(
            act,
            oq[:, :, head * 256 : (head + 1) * 256].reshape(640, 256),
            preferred_element_type=F32,
        )
        query_lin_out[:, head * 256 : (head + 1) * 256] = lin
        row = turned(lin, gains[1:2, :256])
        query_out[head * 64 : (head + 1) * 64] = row[:64]
        query_out[256 + head * 64 : 256 + (head + 1) * 64] = row[64:]

    for gather in (keys, values):
        gather.middle(xl)
    for gather in (keys, values):
        gather.middle(1 - xl)
    a2.finish()
    b2.finish()
    swap(g.at[:, cols(core * 1024, 1024)])
    swap(u.at[:, cols(core * 1024, 1024)])
    swap(w.at[rows(core, 256)])
    direct_d.wait_recv()
    swap(half_d(d))
    for k in range(8):
        for gather in (keys, values):
            gather.relay(k)
    for k in range(8):
        for gather in (keys, values):
            gather.finish(k)
    for ring in (kv1, kv2, a1, b1, a2, b2, keys, values):
        ring.drain()
    for copy in crosses + [direct_q, direct_d, swap_q] + first:
        copy.wait_send()
    for copy in swaps:
        copy.wait()


def front(weights, inputs, gains, cosine, sine):
    wq, wk, wv, wo, wg, wu, wd = weights
    full = lambda rows, width: pltpu.VMEM((2, rows, width), BF16)
    kv = pltpu.VMEM((2, 4, 4, 2, 128, 256), BF16)
    count = 4 + 2 + 2 + 4 * (2 + 4 + 2) + 2 * (2 + 8) * 4 + 2 * 8 * 4 + 5
    outs = pl.pallas_call(
        front_kernel,
        name="front",
        out_shape=(
            full(320, 1024), full(320, 512), full(512, 640), full(320, 2048), full(320, 2048),
            full(1024, 640), kv, kv,
            jax.ShapeDtypeStruct((128, 640), BF16),
            jax.ShapeDtypeStruct((128, 1024), F32),
            jax.ShapeDtypeStruct((128, 256), F32),
            jax.ShapeDtypeStruct((512, 256), BF16),
        ),
        in_specs=[HBM] * 7 + [VMEM] * 4,
        out_specs=(VMEM,) * 12,
        scratch_shapes=[
            pltpu.SemaphoreType.DMA((count,)),
            pltpu.SemaphoreType.DMA((count,)),
            pltpu.SemaphoreType.DMA((7,)),
        ],
        compiler_params=pltpu.CompilerParams(
            collective_id=1, has_side_effects=True, vmem_limit_bytes=16 << 20
        ),
    )(*[pltpu.with_memory_space_constraint(w, pltpu.HBM) for w in weights], inputs, gains, cosine, sine)
    flat = [o.reshape(2 * o.shape[1], o.shape[2]) for o in outs[:6]]
    return flat + [o.reshape(64, 128, 256) for o in outs[6:8]] + list(outs[8:])


def add_into(dst, src):
    dst[...] = dst[...] + src[...]


def sum_into(dst, terms):
    total = terms[0][...].astype(dst.dtype)
    for t in terms[1:]:
        total = total + t[...].astype(dst.dtype)
    dst[...] = total


class SumRing:
    def __init__(self, links, axis, me, block, half, pass0, pass1, from_left, from_right, part):
        self.links = links
        self.me, self.left, self.right, self.far = me, (me + 3) % 4, (me + 1) % 4, (me + 2) % 4
        self.to_left, self.to_right = axis_neighbour(axis, 3), axis_neighbour(axis, 1)
        self.block, self.half = block, half
        self.pass0, self.pass1 = pass0, pass1
        self.from_left, self.from_right = from_left, from_right
        self.part = part

    def start(self, ready):
        send = self.links.send
        ready(self.far)
        self.a = send(self.half(self.far, 0), self.pass0, self.to_right)
        self.b = send(self.half(self.far, 1), self.pass1, self.to_left)
        ready(self.right)
        self.c = send(self.half(self.right, 1), self.part(self.from_left, 1), self.to_right)
        ready(self.left)
        self.d = send(self.half(self.left, 0), self.part(self.from_right, 0), self.to_left)
        ready(self.me)

    def relay(self):
        send = self.links.send
        self.a.wait_recv()
        add_into(self.half(self.right, 0), self.pass0)
        self.e = send(self.half(self.right, 0), self.part(self.from_left, 0), self.to_right)
        self.b.wait_recv()
        add_into(self.half(self.left, 1), self.pass1)
        self.f = send(self.half(self.left, 1), self.part(self.from_right, 1), self.to_left)

    def finish(self, out):
        for copy in (self.c, self.d, self.e, self.f):
            copy.wait_recv()
        sum_into(out, [self.block(self.me), self.from_left, self.from_right])

    def drain(self):
        for copy in (self.a, self.b, self.c, self.d, self.e, self.f):
            copy.wait_send()


class Direct:
    def __init__(self, links, axis, me, block, got):
        self.links, self.axis, self.me, self.block, self.got = links, axis, me, block, got

    def start(self):
        self.copies = [
            self.links.send(
                self.block((self.me + step) % 4), self.got.at[step - 1], axis_neighbour(self.axis, step)
            )
            for step in (1, 2, 3)
        ]

    def finish(self, out):
        for copy in self.copies:
            copy.wait_recv()
        sum_into(out, [self.block(self.me)] + [self.got.at[i] for i in range(3)])

    def drain(self):
        for copy in self.copies:
            copy.wait_send()


def nothing(i):
    pass


class KeySum:
    SCRATCH = 12

    def __init__(self, links, source, out, scratch, axes):
        h, xl, z, y, core = place()
        self.links, self.source, self.out, self.axes = links, source, out, axes
        self.xl, self.core, self.me = xl, core, {"y": y, "z": z}
        self.got, self.p0, self.p1, self.fl, self.fr, self.second, self.q0, self.q1, self.gl, self.gr, self.third, self.last = scratch
        self.other = device(h, 1 - xl, z, y, core)

    @staticmethod
    def scratch():
        buf = lambda *lead: pltpu.VMEM(lead + (128, 256), BF16)
        return [buf(2, 4, 4), buf(4), buf(4), buf(2, 4), buf(2, 4), buf(2, 4), buf(), buf(), buf(2), buf(2), buf(2), buf()]

    def at(self, ref, i, *more):
        return ref.at[(slice(None), i, slice(None)) + more] if self.axes[0] == "z" else ref.at[(slice(None), slice(None), i) + more]

    def swap(self):
        me = self.me[self.axes[0]]
        self.swaps = [
            self.links.send(self.at(self.source, i, 1 - self.core), self.at(self.got, i), sibling())
            for i in ((me + 2) % 4, (me + 1) % 4, (me + 3) % 4, me)
        ]
        self.pending = list(self.swaps)

    def ready(self, i):
        self.pending.pop(0).wait_recv()
        mine, got = self.at(self.source, i, self.core), self.at(self.got, i)
        add_into(got, mine)

    def start(self):
        first, second = self.axes
        half = lambda i, k: self.got.at[(k, i) if first == "z" else (k, slice(None), i)]
        self.ring = SumRing(
            self.links, first, self.me[first], lambda i: self.at(self.got, i), half,
            self.p0, self.p1, self.fl, self.fr, lambda ref, k: ref.at[k],
        )
        self.ring2 = SumRing(
            self.links, second, self.me[second], lambda i: self.second.at[:, i],
            lambda i, k: self.second.at[k, i],
            self.q0, self.q1, self.gl, self.gr, lambda ref, k: ref.at[k],
        )
        self.ring.start(self.ready)

    def relay(self):
        self.ring.relay()

    def next(self):
        self.ring.finish(self.second)
        self.ring2.start(nothing)

    def relay2(self):
        self.ring2.relay()

    def next2(self):
        self.ring2.finish(self.third)
        self.copy = self.links.send(self.third.at[1 - self.xl], self.last, self.other)

    def finish(self):
        self.copy.wait_recv()
        self.out[...] = self.third[self.xl].astype(F32) + self.last[...].astype(F32)

    def drain(self):
        self.ring.drain()
        self.ring2.drain()
        for copy in self.swaps + [self.copy]:
            copy.wait_send()


SIZES = {"xl": 2, "z": 4, "y": 4, "xh": 2}


def pick(ref, dims, axis, i, core=None):
    spot, left = [], []
    for name in dims:
        if axis == "x" and name == "xl":
            spot.append(i % 2)
        elif axis == "x" and name == "xh":
            spot.append(i // 2)
        elif name == axis:
            spot.append(i)
        else:
            spot.append(slice(None))
            left.append(name)
        if core is not None and name == "y":
            spot.append(core)
    return ref.at[tuple(spot)], tuple(left)


def without(dims, axis):
    return tuple(n for n in dims if not n.startswith(axis))


def sizes(dims):
    return tuple(SIZES[n] for n in dims)


def first_half(ref, k):
    n = ref.shape[0] // 2
    return ref.at[pl.ds(n * k, n)]


class WeightSum:
    SCRATCH = 12
    DIMS = ("xl", "z", "y", "xh")

    def __init__(self, links, source, out, scratch, axes):
        h, xl, z, y, core = place()
        self.links, self.source, self.out, self.axes = links, source, out, axes
        self.core, self.me = core, {"x": 2 * h + xl, "y": y, "z": z}
        (
            self.got, self.p0, self.p1, self.fl, self.fr,
            self.total2, self.q0, self.q1, self.gl, self.gr, self.total3, self.last,
        ) = scratch
        self.dims2 = without(self.DIMS, axes[0])
        self.dims3 = without(self.dims2, axes[1])

    @classmethod
    def scratch(cls, rows, axes):
        buf = lambda *lead: pltpu.VMEM(lead + (rows, 128), BF16)
        two = without(cls.DIMS, axes[0])
        three = without(two, axes[1])
        a, b = sizes(two), sizes(three)
        half_a, half_b = (a[0] // 2,) + a[1:], (b[0] // 2,) + b[1:]
        return (
            [buf(*sizes(cls.DIMS)), buf(*half_a), buf(*half_a), buf(*a), buf(*a)]
            + [buf(*a), buf(*half_b), buf(*half_b), buf(*b), buf(*b)]
            + [buf(*b), buf(3)]
        )

    def mine(self, i, core):
        return pick(self.source, self.DIMS, self.axes[0], i, core)[0]

    def block(self, i):
        return pick(self.got, self.DIMS, self.axes[0], i)[0]

    def block2(self, i):
        return pick(self.total2, self.dims2, self.axes[1], i)[0]

    def block3(self, i):
        return pick(self.total3, self.dims3, self.axes[2], i)[0]

    def swap(self):
        me = self.me[self.axes[0]]
        self.swaps = [
            self.links.send(self.mine(i, 1 - self.core), self.block(i), sibling())
            for i in ((me + 2) % 4, (me + 1) % 4, (me + 3) % 4, me)
        ]
        self.pending = list(self.swaps)

    def ready(self, i):
        self.pending.pop(0).wait_recv()
        add_into(self.block(i), self.mine(i, self.core))

    def start(self):
        first, second, third = self.axes
        self.ring = SumRing(
            self.links, first, self.me[first], self.block,
            lambda i, k: first_half(self.block(i), k),
            self.p0, self.p1, self.fl, self.fr, first_half,
        )
        self.ring2 = SumRing(
            self.links, second, self.me[second], self.block2,
            lambda i, k: first_half(self.block2(i), k),
            self.q0, self.q1, self.gl, self.gr, first_half,
        )
        self.direct = Direct(self.links, third, self.me[third], self.block3, self.last)
        self.ring.start(self.ready)

    def relay(self):
        self.ring.relay()

    def next(self):
        self.ring.finish(self.total2)
        self.ring2.start(nothing)

    def relay2(self):
        self.ring2.relay()

    def next2(self):
        self.ring2.finish(self.total3)
        self.direct.start()

    def finish(self):
        self.direct.finish(self.out)

    def drain(self):
        self.ring.drain()
        self.ring2.drain()
        self.direct.drain()
        for copy in self.swaps:
            copy.wait_send()


def tile(ref, inverse, step):
    parts = []
    for j in range(8):
        block = step * 8 + j
        late = block >= 64
        owner = inverse[jnp.where(late, 127 - block, block)]
        half = pl.multiple_of(jnp.where(late, 64, 0), 64)
        parts.append(ref[owner, pl.ds(half, 64), :])
    return jnp.concatenate(parts, axis=0)


def attend(own, inverse, query, keys, values, acc, weight):
    acc[...] = jnp.zeros_like(acc)
    weight[...] = jnp.zeros_like(weight)

    def step_for(part, block, step, masked):
        here = pl.ds(part * 256, 256)
        k = tile(keys, inverse, step)
        v = tile(values, inverse, step)
        raw = lax.dot_general(query[here, :], k, NT, preferred_element_type=F32)
        p = jnp.exp2(raw * EXP2_SCALE)
        if masked:
            token = lax.broadcasted_iota(jnp.int32, (256, 512), 0) % 64 + block * 64
            position = lax.broadcasted_iota(jnp.int32, (256, 512), 1) + step * 512
            p = jnp.where(position <= token, p, 0.0)
        weight[here, :] += p[:, :128] + p[:, 128:256] + p[:, 256:384] + p[:, 384:]
        acc[here, :] += jnp.dot(p.astype(BF16), v, preferred_element_type=F32)

    for part in range(2):
        block = own if part == 0 else 127 - own
        full = block // 8

        @pl.loop(0, full)
        def _(step):
            step_for(part, block, step, False)

        step_for(part, block, full, True)


def attend_back(own, inverse, query, d_out, log_sum, delta, keys, values, d_query, d_keys, d_values):
    d_query[...] = jnp.zeros_like(d_query)

    def terms(part, step, k, v, masked):
        rows = pl.ds(part * 256, 256)
        block = own if part == 0 else 127 - own
        q = query[rows, :]
        g = d_out[rows, :]
        raw = lax.dot_general(k, q, NT, preferred_element_type=F32)
        p = jnp.exp2(raw * EXP2_SCALE - log_sum[:, part * 256 : (part + 1) * 256])
        if masked:
            position = lax.broadcasted_iota(jnp.int32, (512, 256), 0) + step * 512
            token = lax.broadcasted_iota(jnp.int32, (512, 256), 1) % 64 + block * 64
            p = jnp.where(position <= token, p, 0.0)
        d_p = lax.dot_general(v, g, NT, preferred_element_type=F32)
        d_s = (p * (d_p - delta[:, part * 256 : (part + 1) * 256])).astype(BF16)
        d_query[rows, :] += lax.dot_general(d_s, k, TN, preferred_element_type=F32)
        d_k = jnp.dot(d_s, q, preferred_element_type=F32)
        d_v = jnp.dot(p.astype(BF16), g, preferred_element_type=F32)
        return d_k, d_v

    def store(step, d_k, d_v):
        for j in range(8):
            block = step * 8 + j
            late = block >= 64
            owner = inverse[jnp.where(late, 127 - block, block)]
            half = pl.multiple_of(jnp.where(late, 64, 0), 64)
            d_keys[owner, pl.ds(half, 64), :] = (d_k[j * 64 : (j + 1) * 64] * SCALE).astype(BF16)
            d_values[owner, pl.ds(half, 64), :] = d_v[j * 64 : (j + 1) * 64].astype(BF16)

    early_full = own // 8
    late_full = (127 - own) // 8

    @pl.loop(0, early_full)
    def _(step):
        k = tile(keys, inverse, step)
        v = tile(values, inverse, step)
        d_k, d_v = terms(1, step, k, v, False)
        d_k2, d_v2 = terms(0, step, k, v, False)
        store(step, d_k + d_k2, d_v + d_v2)

    k = tile(keys, inverse, early_full)
    v = tile(values, inverse, early_full)
    d_k, d_v = terms(1, early_full, k, v, False)
    d_k2, d_v2 = terms(0, early_full, k, v, True)
    store(early_full, d_k + d_k2, d_v + d_v2)

    @pl.loop(early_full + 1, late_full)
    def _(step):
        d_k, d_v = terms(1, step, tile(keys, inverse, step), tile(values, inverse, step), False)
        store(step, d_k, d_v)

    d_k, d_v = terms(
        1, late_full, tile(keys, inverse, late_full), tile(values, inverse, late_full), True
    )
    store(late_full, d_k, d_v)
    zero = jnp.zeros((512, 256), F32)

    @pl.loop(late_full + 1, 16)
    def _(step):
        store(step, zero, zero)

    d_query[...] = d_query[...] * SCALE


def dot(a, b):
    return jnp.dot(a, b, preferred_element_type=F32)


def dot_nt(a, b):
    return lax.dot_general(a, b, NT, preferred_element_type=F32)


def dot_tn(a, b):
    return lax.dot_general(a, b, TN, preferred_element_type=F32)


def norm_back(values, gain, d_out):
    r = lax.rsqrt(jnp.mean(values * values, axis=-1, keepdims=True) + EPS)
    n = values * r
    d_gain = jnp.sum(d_out * n, axis=0, keepdims=True)
    d_n = d_out * gain
    return r * (d_n - n * jnp.mean(d_n * n, axis=-1, keepdims=True)), d_gain


def gelu_terms(x):
    c = math.sqrt(2.0 / math.pi)
    square = x * x
    t = jnp.tanh(c * x * (1.0 + 0.044715 * square))
    half = 0.5 * (1.0 + t)
    slope = half + 0.5 * x * (1.0 - t * t) * c * (1.0 + 3 * 0.044715 * square)
    return x * half, slope


def by_fives(act):
    i = lax.broadcasted_iota(jnp.int32, (640, 640), 0)
    j = lax.broadcasted_iota(jnp.int32, (640, 640), 1)
    chosen = (i == 5 * (j % 128) + j // 128).astype(F32).astype(BF16)
    return dot(act, chosen).astype(BF16)


def spread_rows(flat, act, grad, rows, first=0):
    tiles = grad.shape[1] // 128
    for t in range(5):
        part = dot_tn(act[:, t * 128 : (t + 1) * 128], grad)
        for c in range(tiles):
            flat[pl.ds(first + t * tiles + c, 128, stride=rows), :] = part[
                :, c * 128 : (c + 1) * 128
            ]


def pack(out, flat, rows):
    @pl.loop(0, 128)
    def _(i):
        out[i] = flat[pl.ds(pl.multiple_of(i * rows, 8), rows), :].astype(BF16)


def middle_kernel(
    inverse, pair, query, keys, values, inputs, cotangent, wo, wg, wu, wd, gains,
    layer_out, grad_resid_out, d_query, d_keys, d_values, gr_down, gr_gate, gr_up, gr_out, gr_gains,
    acc, weight, gate, upper, hidden, d_gate, d_upper, att, d_att_rows, flat,
):
    own = pair[0]
    attend(own, inverse, query, keys, values, acc, weight)
    attended = acc[...] / jnp.sum(weight[...], axis=1, keepdims=True)
    acc[...] = attended
    ones = jnp.ones((8, 128), F32)
    sums = lax.dot_general(
        ones, weight[...], NT, precision=lax.Precision.HIGHEST, preferred_element_type=F32
    )
    log_sum = jnp.log2(sums[:1])
    attended = attended.astype(BF16)
    for b in range(2):
        for head in range(4):
            att[b * 64 : (b + 1) * 64, head * 256 : (head + 1) * 256] = attended[
                b * 256 + head * 64 : b * 256 + (head + 1) * 64
            ]

    att_lin = dot(att[...], wo[...])
    resid = inputs[...].astype(F32) + norm_scale(att_lin, gains[3:4])
    act_two = norm_scale(resid, gains[4:5]).astype(BF16)
    for c in range(4):
        s = slice(c * 512, (c + 1) * 512)
        gate[:, s] = dot(act_two, wg[:, s])
        upper[:, s] = dot(act_two, wu[:, s])
        hidden[:, s] = (gelu_terms(gate[:, s])[0] * upper[:, s]).astype(BF16)
    down = dot(hidden[...], wd[...])
    layer_out[...] = (resid + norm_scale(down, gains[5:6])).astype(BF16)

    grad_y = cotangent[...].astype(F32)
    d_down, d_post_ff = norm_back(down, gains[5:6], grad_y)
    d_down = d_down.astype(BF16)
    d_act_two = jnp.zeros((128, 640), F32)
    for c in range(4):
        s = slice(c * 512, (c + 1) * 512)
        d_hidden = dot_nt(d_down, wd[s, :])
        value, slope = gelu_terms(gate[:, s])
        a = (d_hidden * upper[:, s] * slope).astype(BF16)
        b = (d_hidden * value).astype(BF16)
        d_gate[:, s] = a
        d_upper[:, s] = b
        d_act_two = d_act_two + dot_nt(a, wg[:, s]) + dot_nt(b, wu[:, s])
    d_resid, d_pre_ff = norm_back(resid, gains[4:5], d_act_two)
    grad_resid = grad_y + d_resid
    grad_resid_out[...] = grad_resid
    d_att, d_post_attn = norm_back(att_lin, gains[3:4], grad_resid)
    d_att = d_att.astype(BF16)
    gr_gains[...] = jnp.concatenate(
        [d_post_attn, d_pre_ff, d_post_ff, jnp.zeros((5, 640), F32)], axis=0
    )
    d_attended = dot_nt(d_att, wo[...]).astype(BF16)
    for b in range(2):
        for head in range(4):
            d_att_rows[b * 256 + head * 64 : b * 256 + (head + 1) * 64] = d_attended[
                b * 64 : (b + 1) * 64, head * 256 : (head + 1) * 256
            ]
    delta = lax.dot_general(
        jnp.ones((8, 256), F32),
        d_att_rows[...].astype(F32) * acc[...],
        NT,
        precision=lax.Precision.HIGHEST,
        preferred_element_type=F32,
    )[:1]

    @pl.loop(0, 16)
    def _(i):
        part = dot_tn(hidden[:, pl.ds(pl.multiple_of(i * 128, 128), 128)], d_down).astype(BF16)
        for j in range(8):
            for c in range(5):
                gr_down[i * 8 + j, c * 16 : (c + 1) * 16, :] = part[
                    j * 16 : (j + 1) * 16, c * 128 : (c + 1) * 128
                ]

    @pl.loop(0, 8)
    def _(i):
        part = dot_tn(att[:, pl.ds(pl.multiple_of(i * 128, 128), 128)], d_att)
        for j in range(16):
            rows = part[j * 8 : (j + 1) * 8]
            gr_out[i * 16 + j] = jnp.concatenate(
                [rows[:, c * 128 : (c + 1) * 128] for c in range(5)], axis=0
            ).astype(BF16)

    fives = by_fives(act_two)
    spread_rows(flat, fives, d_gate[...], 80)
    pack(gr_gate, flat, 80)
    spread_rows(flat, fives, d_upper[...], 80)
    pack(gr_up, flat, 80)

    attend_back(
        own, inverse, query, d_att_rows, log_sum, delta, keys, values, d_query, d_keys, d_values
    )


def middle(*args):
    block = lambda rows: pltpu.VMEM((128, rows, 128), BF16)
    kv = pltpu.VMEM((64, 128, 256), BF16)
    return pl.pallas_call(
        middle_kernel,
        name="middle",
        out_shape=(
            jax.ShapeDtypeStruct((128, 640), BF16),
            jax.ShapeDtypeStruct((128, 640), F32),
            jax.ShapeDtypeStruct((512, 256), F32),
            kv, kv, block(80), block(80), block(80), block(40),
            jax.ShapeDtypeStruct((8, 640), F32),
        ),
        in_specs=[SMEM, SMEM] + [VMEM] * 10,
        out_specs=(VMEM,) * 10,
        scratch_shapes=[
            pltpu.VMEM((512, 256), F32),
            pltpu.VMEM((512, 128), F32),
            pltpu.VMEM((128, 2048), F32),
            pltpu.VMEM((128, 2048), F32),
            pltpu.VMEM((128, 2048), BF16),
            pltpu.VMEM((128, 2048), BF16),
            pltpu.VMEM((128, 2048), BF16),
            pltpu.VMEM((128, 1024), BF16),
            pltpu.VMEM((512, 256), BF16),
            pltpu.VMEM((128 * 80, 128), F32),
        ],
        compiler_params=pltpu.CompilerParams(vmem_limit_bytes=23 << 20),
    )(*args)


FIRST_ROWS, FIRST_ORDERS = (80, 80, 80, 40), ("xyz", "xzy", "yzx", "zxy")
LAST_ROWS, LAST_ORDERS = (40, 32), ("xyz", "yzx")


def pack_places(out, flat, rows):
    @pl.loop(0, 128)
    def _(i):
        out[i // 64, (i // 16) % 4, (i // 4) % 4, (i // 2) % 2, i % 2] = flat[
            pl.ds(pl.multiple_of(i * rows, 8), rows), :
        ].astype(BF16)


def project_back(
    d_query, d_key, d_value, query_lin, key_lin, act_one, inputs, wq, wkv, gains, cosine, sine, grad_resid, d_gains,
    input_grad, gr_query, gr_tail,
    d_query_lin, d_kv_lin, flat, flat_tail,
):
    cos, sin = cosine[...], sine[...]

    def turn_back(lin, gain, grad):
        a, b = grad[:, :128], grad[:, 128:]
        d_n = jnp.concatenate([a * cos + b * sin, b * cos - a * sin], axis=1)
        return norm_back(lin, gain, d_n)

    fives = by_fives(act_one[...])
    d_gain_query = jnp.zeros((1, 256), F32)
    for head in range(4):
        cut = slice(head * 256, (head + 1) * 256)
        grad = jnp.concatenate(
            [d_query[b * 256 + head * 64 : b * 256 + (head + 1) * 64] for b in range(2)], axis=0
        )
        d_lin, d_gain = turn_back(query_lin[:, cut], gains[1:2, :256], grad)
        d_query_lin[:, cut] = d_lin.astype(BF16)
        d_gain_query = d_gain_query + d_gain
    spread_rows(flat, fives, d_query_lin[...], 40)
    pack_places(gr_query, flat, 40)
    d_act = dot_nt(d_query_lin[...], wq[...])
    yield
    d_lin, d_gain_key = turn_back(key_lin[...], gains[2:3, :256], d_key[...])
    d_kv_lin[:, :256] = d_lin.astype(BF16)
    d_kv_lin[:, 256:] = d_value[...].astype(BF16)
    d_act = d_act + dot_nt(d_kv_lin[...], wkv[...])
    d_states, d_gain_in = norm_back(inputs[...].astype(F32), gains[0:1], d_act)
    input_grad[...] = (grad_resid[...] + d_states).astype(BF16)
    flat_tail[...] = jnp.zeros_like(flat_tail)
    spread_rows(flat_tail, fives, d_kv_lin[...], 32)
    total = jnp.zeros((128, 128), F32)
    column = 0
    for row, each in (
        (d_gain_in, 5),
        (d_gains[0:1], 5),
        (d_gains[1:2], 5),
        (d_gains[2:3], 5),
        (d_gain_query, 2),
        (d_gain_key, 2),
    ):
        n = 128 * each
        owner = lax.broadcasted_iota(jnp.int32, (128, n), 1) // each
        mine = owner == lax.broadcasted_iota(jnp.int32, (128, n), 0)
        spot = lax.broadcasted_iota(jnp.int32, (n, 128), 0) % each + column
        here = spot == lax.broadcasted_iota(jnp.int32, (n, 128), 1)
        total = total + dot(
            jnp.where(mine, row, 0.0).astype(BF16), here.astype(F32).astype(BF16)
        )
        column += each
    flat_tail[pl.ds(20, 128, stride=32), :] = total
    pack_places(gr_tail, flat_tail, 32)
    yield


def back_kernel(*refs):
    refs = list(refs)

    def take(n):
        some = refs[:n]
        del refs[:n]
        return some

    kv_sources, first_sources, others = take(2), take(4), take(12)
    input_grad, o_query, o_key, o_value, o_output, o_gate, o_up, o_down, o_gains = take(9)
    kv_sums = take(2)
    first_sums, last_sources, last_sums, temps = take(4), take(2), take(2), take(4)
    kv_scratch = [take(KeySum.SCRATCH) for _ in range(2)]
    first_scratch = [take(WeightSum.SCRATCH) for _ in range(4)]
    last_scratch = [take(WeightSum.SCRATCH) for _ in range(2)]
    send_sems, recv_sems = refs
    greet(
        [sibling()] + [axis_neighbour(a, s) for a in ("x", "y", "z") for s in (1, 2, 3)]
    )
    links = Links(send_sems, recv_sems)
    kv = [
        KeySum(links, *args)
        for args in zip(kv_sources, kv_sums, kv_scratch, ("zy", "yz"))
    ]
    first = [
        WeightSum(links, *args)
        for args in zip(first_sources, first_sums, first_scratch, FIRST_ORDERS)
    ]
    final = [
        WeightSum(links, *args)
        for args in zip(last_sources, last_sums, last_scratch, LAST_ORDERS)
    ]

    def run(group, *stages):
        for stage in stages:
            for s in group:
                getattr(s, stage)()

    d_query, query_lin = others[:2]
    projections = project_back(
        d_query, *kv_sums, *others[1:], input_grad, *last_sources, *temps
    )
    run(kv, "swap")
    run(first, "swap")
    run(kv, "start")
    run(first, "start")
    next(projections)
    run(kv, "relay")
    run(first, "relay")
    run(kv, "next", "relay2", "next2")
    run(first, "next")
    run(kv, "finish")
    next(projections)
    run(final, "swap", "start")
    run(first, "relay2", "next2")
    run(final, "relay", "next", "relay2", "next2")
    run(first, "finish")
    run(final, "finish")
    run(kv + first + final, "drain")

    s_down, s_gate, s_up, s_output = first_sums
    s_query, s_tail = last_sums
    for c in range(5):
        cut = slice(c * 128, (c + 1) * 128)
        o_down[:, cut] = s_down[c * 16 : (c + 1) * 16, :]
        o_output[:, cut] = s_output[c * 8 : (c + 1) * 8, :]
    for out, source, first_row, step, tiles in (
        (o_gate, s_gate, 0, 16, 16),
        (o_up, s_up, 0, 16, 16),
        (o_query, s_query, 0, 8, 8),
        (o_key, s_tail, 0, 4, 2),
        (o_value, s_tail, 2, 4, 2),
    ):
        for c in range(tiles):
            out[:, c * 128 : (c + 1) * 128] = source[pl.ds(first_row + c, 5, stride=step), :]
    o_gains[...] = s_tail[20:21, :]


def back(kv, grads, others):
    buf = lambda *shape: pltpu.VMEM(shape, F32)
    scratch = [buf(128, 256)] * 2
    scratch += [buf(rows, 128) for rows in FIRST_ROWS]
    scratch += [pltpu.VMEM((2, 4, 4, 2, 2, rows, 128), BF16) for rows in LAST_ROWS]
    scratch += [buf(rows, 128) for rows in LAST_ROWS]
    scratch += [
        pltpu.VMEM((128, 1024), BF16),
        pltpu.VMEM((128, 512), BF16),
        buf(128 * 40, 128),
        buf(128 * 32, 128),
    ]
    for _ in kv:
        scratch += KeySum.scratch()
    for rows, order in zip(FIRST_ROWS + LAST_ROWS, FIRST_ORDERS + LAST_ORDERS):
        scratch += WeightSum.scratch(rows, order)
    count = 2 * 17 + 6 * 19
    out = lambda rows, width: jax.ShapeDtypeStruct((rows, width), F32)
    return pl.pallas_call(
        back_kernel,
        name="back",
        out_shape=(
            jax.ShapeDtypeStruct((128, 640), BF16),
            out(5, 1024), out(5, 256), out(5, 256), out(8, 640), out(5, 2048), out(5, 2048),
            out(16, 640), out(1, 128),
        ),
        in_specs=[VMEM] * 18,
        out_specs=(VMEM,) * 9,
        scratch_shapes=scratch
        + [pltpu.SemaphoreType.DMA((count,)), pltpu.SemaphoreType.DMA((count,))],
        compiler_params=pltpu.CompilerParams(
            collective_id=2, has_side_effects=True, vmem_limit_bytes=36 << 20
        ),
    )(
        *[g.reshape((2, 4, 4, 2) + g.shape[1:]) for g in kv],
        *[g.reshape((2, 4, 4, 2, 2) + g.shape[1:]) for g in grads],
        *others,
    )


def local(
    inputs,
    pair_order,
    w_query,
    w_key,
    w_value,
    w_output,
    w_gate,
    w_up,
    w_down,
    gain_in,
    gain_query,
    gain_key,
    gain_post_attn,
    gain_pre_ff,
    gain_post_ff,
    cotangent,
):
    rows = 128
    me_index = lax.axis_index("ctx")
    own_pair = lax.dynamic_slice_in_dim(pair_order, me_index, 1)
    within = jnp.arange(rows, dtype=jnp.int32)
    block_id = jnp.where(within < 64, own_pair, 127 - own_pair)
    positions = block_id * 64 + within % 64
    freq = ROPE_BASE ** (-jnp.arange(128, dtype=F32) / 128)
    angles = positions.astype(F32)[:, None] * freq
    cosine, sine = jnp.cos(angles), jnp.sin(angles)
    matches = pair_order[None, :] == jnp.arange(64, dtype=jnp.int32)[:, None]
    inverse = jnp.sum(jnp.where(matches, jnp.arange(64, dtype=jnp.int32)[None, :], 0), axis=1)
    wide = lambda g: jnp.pad(g, (0, 640 - g.shape[0]))
    gains = jnp.stack(
        [wide(g) for g in (gain_in, gain_query, gain_key, gain_post_attn, gain_pre_ff, gain_post_ff)]
        + [jnp.zeros((640,), F32)] * 2
    )
    (
        wq_all, wkv_all, wo_all, wg_all, wu_all, wd_all, keys, values,
        act_one, query_lin, key_lin, query,
    ) = front(
        (w_query, w_key, w_value, w_output, w_gate, w_up, w_down), inputs[0], gains, cosine, sine
    )
    layer_out, grad_resid, d_query, d_keys, d_values, gr_down, gr_gate, gr_up, gr_out, d_gains = middle(
        inverse, own_pair, query, keys, values, inputs[0], cotangent[0],
        wo_all, wg_all, wu_all, wd_all, gains,
    )
    input_grad, s_query, s_key, s_value, s_output, s_gate, s_up, s_down, s_gains = back(
        (d_keys, d_values), (gr_down, gr_gate, gr_up, gr_out),
        (d_query, query_lin, key_lin, act_one, inputs[0], wq_all, wkv_all, gains, cosine, sine, grad_resid, d_gains),
    )
    s_gains = s_gains[0]
    return (
        layer_out[None],
        input_grad[None],
        s_query,
        s_key,
        s_value,
        s_output,
        s_gate,
        s_up,
        s_down,
        s_gains[0:5],
        s_gains[20:22],
        s_gains[22:24],
        s_gains[5:10],
        s_gains[10:15],
        s_gains[15:20],
    )


def solution(mesh):
    placed = (
        P("fsdp", "ctx", None),
        P(),
        P("fsdp", None),
        P("fsdp", None),
        P("fsdp", None),
        P("fsdp", None),
        P("fsdp", None),
        P("fsdp", None),
        P("fsdp", None),
        P(),
        P(),
        P(),
        P(),
        P(),
        P(),
        P("fsdp", "ctx", None),
    )
    both = ("ctx", "fsdp")
    return jax.shard_map(
        local,
        mesh=mesh,
        in_specs=placed,
        out_specs=(P("fsdp", "ctx", None),) * 2 + (P(both, None),) * 7 + (P(both),) * 6,
        check_vma=False,
    )
```

```python
import functools
import math

import jax
import jax.numpy as jnp
from jax import lax
from jax.experimental import pallas as pl
from jax.experimental.pallas import tpu as pltpu
from jax.sharding import PartitionSpec as P

EPS = 1e-06
ROPE_BASE = 1000000.0
SCALE = 0.0625
EXP2_SCALE = SCALE * math.log2(math.e)
MESH = pl.DeviceIdType.MESH
BF16 = jnp.bfloat16
F32 = jnp.float32
ANY = pl.BlockSpec(memory_space=pl.ANY)
VMEM = pl.BlockSpec(memory_space=pltpu.VMEM)
HBM = pl.BlockSpec(memory_space=pltpu.HBM)
SMEM = pl.BlockSpec(memory_space=pltpu.SMEM)
NT = (((1,), (1,)), ((), ()))
TN = (((0,), (0,)), ((), ()))


def norm_scale(values, gain):
    return values * lax.rsqrt(jnp.mean(values * values, axis=-1, keepdims=True) + EPS) * gain


def place():
    c = lax.axis_index("ctx")
    h = lax.axis_index("fsdp")
    return h, c // 32, (c // 8) % 4, (c // 2) % 4, c % 2


def device(h, xl, z, y, core):
    return {"ctx": xl * 32 + z * 8 + y * 2 + core, "fsdp": h}


def axis_neighbour(axis, step):
    h, xl, z, y, core = place()
    if axis == "x":
        x = (2 * h + xl + step) % 4
        return device(x // 2, x % 2, z, y, core)
    if axis == "y":
        return device(h, xl, z, (y + step) % 4, core)
    return device(h, xl, (z + step) % 4, y, core)


def sibling():
    h, xl, z, y, core = place()
    return device(h, xl, z, y, 1 - core)


def greet(devices):
    barrier = pltpu.get_barrier_semaphore()
    for d in devices:
        pl.semaphore_signal(barrier, inc=1, device_id=d, device_id_type=MESH)
    pl.semaphore_wait(barrier, len(devices))


class Links:
    def __init__(self, send_sems, recv_sems):
        self.send_sems, self.recv_sems, self.count = send_sems, recv_sems, 0

    def send(self, src, dst, target):
        i = self.count
        self.count += 1
        assert i < self.send_sems.shape[0]
        copy = pltpu.make_async_remote_copy(
            src_ref=src,
            dst_ref=dst,
            send_sem=self.send_sems.at[i],
            recv_sem=self.recv_sems.at[i],
            device_id=target,
            device_id_type=MESH,
        )
        copy.start()
        return copy


class GatherRing:
    def __init__(self, links, axis, me, items):
        self.links, self.items = links, items
        self.me, self.left, self.right = me, (me + 3) % 4, (me + 1) % 4
        self.to_left, self.to_right = axis_neighbour(axis, 3), axis_neighbour(axis, 1)

    def start(self):
        self.first = []
        for whole, half in self.items:
            mine = whole(self.me)
            self.first.append(
                (
                    self.links.send(mine, mine, self.to_right),
                    self.links.send(mine, mine, self.to_left),
                )
            )

    def relay(self):
        self.second = []
        for (whole, half), (a, b) in zip(self.items, self.first):
            a.wait_recv()
            piece = half(self.left, 0)
            c = self.links.send(piece, piece, self.to_right)
            b.wait_recv()
            piece = half(self.right, 1)
            d = self.links.send(piece, piece, self.to_left)
            self.second.append((c, d))

    def finish(self):
        for c, d in self.second:
            c.wait_recv()
            d.wait_recv()

    def drain(self):
        for pair in self.first + self.second:
            for copy in pair:
                copy.wait_send()


def ring_of(links, axis, me, *items):
    ring = GatherRing(links, axis, me, items)
    ring.start()
    return ring


def gain_row(gains, name):
    first, n = {"in": (0, 5), "post_attn": (5, 5), "pre_ff": (10, 5), "post_ff": (15, 5), "query": (20, 2), "key": (22, 2)}[name]
    return jnp.concatenate([gains[i : i + 1, :] for i in range(first, first + n)], axis=1)


class PairGather:
    def __init__(self, links, axis, me, axis2, me2, piece, swap):
        self.links, self.axis, self.me, self.axis2, self.me2 = links, axis, me, axis2, me2
        self.piece, self.swap = piece, swap
        self.firsts, self.seconds = [], []

    def half(self, ref, k):
        return ref.at[pl.ds(64 * k, 64)]

    def spread(self, p, i):
        here = lambda j: self.piece(p, i, j)
        ring = ring_of(
            self.links, self.axis2, self.me2, (here, lambda j, k: self.half(here(j), k))
        )
        self.swap(here(self.me2))
        self.seconds.append((ring, here))

    def begin(self, p):
        here = lambda i: self.piece(p, i, self.me2)
        self.firsts.append(
            ring_of(self.links, self.axis, self.me, (here, lambda i, k: self.half(here(i), k)))
        )
        self.spread(p, self.me)

    def middle(self, p):
        ring = self.firsts[0 if len(self.seconds) == 2 else 1]
        ring.relay()
        self.spread(p, (self.me + 3) % 4)
        self.spread(p, (self.me + 1) % 4)
        ring.finish()
        self.spread(p, (self.me + 2) % 4)

    def relay(self, k):
        ring, here = self.seconds[k]
        ring.relay()
        self.swap(here((self.me2 + 3) % 4))
        self.swap(here((self.me2 + 1) % 4))

    def finish(self, k):
        ring, here = self.seconds[k]
        ring.finish()
        self.swap(here((self.me2 + 2) % 4))

    def drain(self):
        for ring in self.firsts + [ring for ring, _ in self.seconds]:
            ring.drain()


def front_kernel(
    wq, wk, wv, wo, wg, wu, wd, inputs, gains, cosine, sine,
    oq, okv, oo, og, ou, od, k_all, v_all, act_out, query_lin_out, key_lin_out, query_out,
    send_sems, recv_sems, local_sems,
):
    h, xl, z, y, core = place()
    o = 1 - h
    cross = device(1 - h, 1 - xl, z, y, core)
    other = device(h, 1 - xl, z, y, core)
    locals_ = [
        pltpu.make_async_copy(src, dst, local_sems.at[i])
        for i, (src, dst) in enumerate(
            (
                (wk, okv.at[h, :, pl.ds(0, 256)]),
                (wv, okv.at[h, :, pl.ds(256, 256)]),
                (wq, oq.at[h]),
                (wo, oo.at[h]),
                (wg, og.at[h]),
                (wd, od.at[h]),
                (wu, ou.at[h]),
            )
        )
    ]
    for copy in locals_[:3]:
        copy.start()
    greet(
        [cross, other, sibling()]
        + [axis_neighbour(a, s) for a in ("y", "z") for s in (1, 3)]
    )
    links = Links(send_sems, recv_sems)

    def rows(i, n):
        return pl.ds(pl.multiple_of(i * n, 16), n)

    def cols(start, n):
        return pl.ds(pl.multiple_of(start, 128), n)

    def piece_g(ref, yy, zz):
        return ref.at[rows(yy, 80), cols(core * 1024 + zz * 256, 256)]

    def piece_o(ref, yy, zz):
        return ref.at[rows((core * 4 + yy) * 4 + zz, 16)]

    half_q = lambda ref: ref.at[:, cols(core * 512, 512)]
    half_d = lambda ref: ref.at[rows(core, 512)]
    half_u = lambda ref: ref.at[:, cols(core * 1024, 1024)]
    half_kv = lambda ref: ref.at[:, cols(core * 256, 256)]
    for copy in locals_[:2]:
        copy.wait()
    direct_kv = links.send(half_kv(okv.at[h]), half_kv(okv.at[h]), cross)
    crosses = [
        links.send(piece_g(wg, y, z), piece_g(og.at[h], y, z), cross),
        links.send(piece_o(wo, y, z), piece_o(oo.at[h], y, z), cross),
    ]
    locals_[2].wait()
    direct_q = links.send(half_q(oq.at[h]), half_q(oq.at[h]), cross)
    for copy in locals_[3:]:
        copy.start()
    g, u, q, d, w, kv = og.at[o], ou.at[o], oq.at[o], od.at[o], oo.at[o], okv.at[o]
    swaps = []

    def swap(piece):
        swaps.append(links.send(piece, piece, sibling()))

    states = inputs[...].astype(F32)
    act = norm_scale(states, gain_row(gains, "in")).astype(BF16)
    act_out[...] = act
    direct_kv.wait_recv()
    swap_kv = links.send(half_kv(kv), half_kv(kv), sibling())
    crosses[0].wait_recv()
    a1 = ring_of(
        links, "y", y,
        (
            lambda i: piece_g(g, i, z),
            lambda i, k: g.at[rows(i, 80), cols(core * 1024 + z * 256 + k * 128, 128)],
        ),
    )
    crosses[1].wait_recv()
    b1 = ring_of(
        links, "z", z,
        (
            lambda i: piece_o(w, y, i),
            lambda i, k: w.at[
                rows((core * 4 + y) * 4 + i, 16), pl.ds(384 * k, 256 if k else 384)
            ],
        ),
    )
    swap_kv.wait_recv()

    kv_lin = jnp.dot(act, okv[...].reshape(640, 512), preferred_element_type=F32)
    key_lin_out[...] = kv_lin[:, :256]
    cos, sin = cosine[...], sine[...]

    def turned(lin, gain):
        n = norm_scale(lin, gain)
        a, b = n[:, :128], n[:, 128:]
        return jnp.concatenate([a * cos - b * sin, b * cos + a * sin], axis=1).astype(BF16)

    k_all[xl, z, y, core] = turned(kv_lin[:, :256], gain_row(gains, "key"))
    v_all[xl, z, y, core] = kv_lin[:, 256:].astype(BF16)
    own = lambda ref: ref.at[xl, z, y, core]
    first = [links.send(own(ref), own(ref), other) for ref in (k_all, v_all)]
    keys = PairGather(links, "y", y, "z", z, lambda p, i, j: k_all.at[p, j, i, core], swap)
    values = PairGather(links, "z", z, "y", y, lambda p, i, j: v_all.at[p, i, j, core], swap)
    keys.begin(xl)
    values.begin(xl)
    locals_[5].wait()
    direct_d = links.send(half_d(od.at[h]), half_d(od.at[h]), cross)
    locals_[6].wait()
    direct_u = links.send(half_u(ou.at[h]), half_u(ou.at[h]), cross)
    a1.relay()
    b1.relay()
    a1.finish()
    a2 = ring_of(
        links, "z", z,
        (
            lambda i: g.at[:, cols(core * 1024 + i * 256, 256)],
            lambda i, k: g.at[pl.ds(160 * k, 160), cols(core * 1024 + i * 256, 256)],
        ),
    )
    b1.finish()
    b2 = ring_of(
        links, "y", y,
        (
            lambda i: w.at[rows(core * 4 + i, 64)],
            lambda i, k: w.at[rows((core * 4 + i) * 2 + k, 32)],
        ),
    )
    for copy, gather in zip(first, (keys, values)):
        copy.wait_recv()
        gather.begin(1 - xl)
    for gather in (keys, values):
        gather.middle(xl)
    for gather in (keys, values):
        gather.middle(1 - xl)
    direct_q.wait_recv()
    swap_q = links.send(half_q(q), half_q(q), sibling())
    a2.relay()
    b2.relay()
    swap_q.wait_recv()
    for head in range(4):
        lin = jnp.dot(
            act,
            oq[:, :, head * 256 : (head + 1) * 256].reshape(640, 256),
            preferred_element_type=F32,
        )
        query_lin_out[:, head * 256 : (head + 1) * 256] = lin
        row = turned(lin, gain_row(gains, "query"))
        query_out[head * 64 : (head + 1) * 64] = row[:64]
        query_out[256 + head * 64 : 256 + (head + 1) * 64] = row[64:]

    a2.finish()
    b2.finish()
    swap(g.at[:, cols(core * 1024, 1024)])
    swap(w.at[rows(core, 256)])
    for k in range(8):
        for gather in (keys, values):
            gather.relay(k)
    for direct, half, ref in ((direct_d, half_d, d), (direct_u, half_u, u)):
        direct.wait_recv()
        swap(half(ref))
    for k in range(8):
        for gather in (keys, values):
            gather.finish(k)
    for ring in (a1, b1, a2, b2, keys, values):
        ring.drain()
    for copy in crosses + [direct_kv, direct_q, direct_d, direct_u, swap_kv, swap_q] + first:
        copy.wait_send()
    for copy in swaps:
        copy.wait()
    for copy in locals_[3:5]:
        copy.wait()


def front(weights, inputs, gains, cosine, sine):
    wq, wk, wv, wo, wg, wu, wd = weights
    full = lambda rows, width: pltpu.VMEM((2, rows, width), BF16)
    kv = pltpu.VMEM((2, 4, 4, 2, 128, 256), BF16)
    count = 2 + 4 + 2 + 4 + 2 + 4 * 4 + 2 * (2 + 8) * 4 + 2 * 8 * 4
    outs = pl.pallas_call(
        front_kernel,
        name="front",
        out_shape=(
            full(320, 1024), full(320, 512), full(512, 640), full(320, 2048), full(320, 2048),
            full(1024, 640), kv, kv,
            jax.ShapeDtypeStruct((128, 640), BF16),
            jax.ShapeDtypeStruct((128, 1024), F32),
            jax.ShapeDtypeStruct((128, 256), F32),
            jax.ShapeDtypeStruct((512, 256), BF16),
        ),
        in_specs=[HBM] * 7 + [VMEM] * 4,
        out_specs=(VMEM,) * 12,
        scratch_shapes=[
            pltpu.SemaphoreType.DMA((count,)),
            pltpu.SemaphoreType.DMA((count,)),
            pltpu.SemaphoreType.DMA((7,)),
        ],
        compiler_params=pltpu.CompilerParams(
            collective_id=1, has_side_effects=True, vmem_limit_bytes=16 << 20
        ),
    )(*[pltpu.with_memory_space_constraint(w, pltpu.HBM) for w in weights], inputs, gains, cosine, sine)
    flat = [o.reshape(2 * o.shape[1], o.shape[2]) for o in outs[:6]]
    return flat + [o.reshape(64, 128, 256) for o in outs[6:8]] + list(outs[8:])


def add_into(dst, src):
    dst[...] = dst[...] + src[...]


def sum_into(dst, terms):
    total = terms[0][...].astype(dst.dtype)
    for t in terms[1:]:
        total = total + t[...].astype(dst.dtype)
    dst[...] = total


class SumRing:
    def __init__(self, links, axis, me, block, half, pass0, pass1, from_left, from_right, part):
        self.links = links
        self.me, self.left, self.right, self.far = me, (me + 3) % 4, (me + 1) % 4, (me + 2) % 4
        self.to_left, self.to_right = axis_neighbour(axis, 3), axis_neighbour(axis, 1)
        self.block, self.half = block, half
        self.pass0, self.pass1 = pass0, pass1
        self.from_left, self.from_right = from_left, from_right
        self.part = part

    def start(self, ready):
        send = self.links.send
        ready(self.far)
        self.a = send(self.half(self.far, 0), self.pass0, self.to_right)
        self.b = send(self.half(self.far, 1), self.pass1, self.to_left)
        ready(self.right)
        self.c = send(self.half(self.right, 1), self.part(self.from_left, 1), self.to_right)
        ready(self.left)
        self.d = send(self.half(self.left, 0), self.part(self.from_right, 0), self.to_left)
        ready(self.me)

    def relay(self):
        send = self.links.send
        self.a.wait_recv()
        add_into(self.half(self.right, 0), self.pass0)
        self.e = send(self.half(self.right, 0), self.part(self.from_left, 0), self.to_right)
        self.b.wait_recv()
        add_into(self.half(self.left, 1), self.pass1)
        self.f = send(self.half(self.left, 1), self.part(self.from_right, 1), self.to_left)

    def finish(self, out):
        for copy in (self.c, self.d, self.e, self.f):
            copy.wait_recv()
        sum_into(out, [self.block(self.me), self.from_left, self.from_right])

    def drain(self):
        for copy in (self.a, self.b, self.c, self.d, self.e, self.f):
            copy.wait_send()


class Direct:
    def __init__(self, links, axis, me, block, got):
        self.links, self.axis, self.me, self.block, self.got = links, axis, me, block, got

    def start(self):
        self.copies = [
            self.links.send(
                self.block((self.me + step) % 4), self.got.at[step - 1], axis_neighbour(self.axis, step)
            )
            for step in (1, 2, 3)
        ]

    def finish(self, out):
        for copy in self.copies:
            copy.wait_recv()
        sum_into(out, [self.block(self.me)] + [self.got.at[i] for i in range(3)])

    def drain(self):
        for copy in self.copies:
            copy.wait_send()


def nothing(i):
    pass


class KeySum:
    SCRATCH = 12

    def __init__(self, links, source, out, scratch, axes):
        h, xl, z, y, core = place()
        self.links, self.source, self.out, self.axes = links, source, out, axes
        self.xl, self.core, self.me = xl, core, {"y": y, "z": z}
        self.got, self.p0, self.p1, self.fl, self.fr, self.second, self.q0, self.q1, self.gl, self.gr, self.third, self.last = scratch
        self.other = device(h, 1 - xl, z, y, core)

    @staticmethod
    def scratch():
        buf = lambda *lead: pltpu.VMEM(lead + (128, 256), BF16)
        return [buf(2, 4, 4), buf(4), buf(4), buf(2, 4), buf(2, 4), buf(2, 4), buf(), buf(), buf(2), buf(2), buf(2), buf()]

    def at(self, ref, i, *more):
        return ref.at[(slice(None), i, slice(None)) + more] if self.axes[0] == "z" else ref.at[(slice(None), slice(None), i) + more]

    def swap(self):
        me = self.me[self.axes[0]]
        self.swaps = [
            self.links.send(self.at(self.source, i, 1 - self.core), self.at(self.got, i), sibling())
            for i in ((me + 2) % 4, (me + 1) % 4, (me + 3) % 4, me)
        ]
        self.pending = list(self.swaps)

    def ready(self, i):
        self.pending.pop(0).wait_recv()
        mine, got = self.at(self.source, i, self.core), self.at(self.got, i)
        add_into(got, mine)

    def start(self):
        first, second = self.axes
        half = lambda i, k: self.got.at[(k, i) if first == "z" else (k, slice(None), i)]
        self.ring = SumRing(
            self.links, first, self.me[first], lambda i: self.at(self.got, i), half,
            self.p0, self.p1, self.fl, self.fr, lambda ref, k: ref.at[k],
        )
        self.ring2 = SumRing(
            self.links, second, self.me[second], lambda i: self.second.at[:, i],
            lambda i, k: self.second.at[k, i],
            self.q0, self.q1, self.gl, self.gr, lambda ref, k: ref.at[k],
        )
        self.ring.start(self.ready)

    def relay(self):
        self.ring.relay()

    def next(self):
        self.ring.finish(self.second)
        self.ring2.start(nothing)

    def relay2(self):
        self.ring2.relay()

    def next2(self):
        self.ring2.finish(self.third)
        self.copy = self.links.send(self.third.at[1 - self.xl], self.last, self.other)

    def finish(self):
        self.copy.wait_recv()
        self.out[...] = self.third[self.xl].astype(F32) + self.last[...].astype(F32)

    def drain(self):
        self.ring.drain()
        self.ring2.drain()
        for copy in self.swaps + [self.copy]:
            copy.wait_send()


SIZES = {"xl": 2, "z": 4, "y": 4, "xh": 2}


def pick(ref, dims, axis, i, core=None):
    spot, left = [], []
    for name in dims:
        if axis == "x" and name == "xl":
            spot.append(i % 2)
        elif axis == "x" and name == "xh":
            spot.append(i // 2)
        elif name == axis:
            spot.append(i)
        else:
            spot.append(slice(None))
            left.append(name)
        if core is not None and name == "y":
            spot.append(core)
    return ref.at[tuple(spot)], tuple(left)


def without(dims, axis):
    return tuple(n for n in dims if not n.startswith(axis))


def sizes(dims):
    return tuple(SIZES[n] for n in dims)


def first_half(ref, k):
    n = ref.shape[0] // 2
    return ref.at[pl.ds(n * k, n)]


class WeightSum:
    SCRATCH = 12
    DIMS = ("xl", "z", "y", "xh")

    def __init__(self, links, source, out, scratch, axes):
        h, xl, z, y, core = place()
        self.links, self.source, self.out, self.axes = links, source, out, axes
        self.core, self.me = core, {"x": 2 * h + xl, "y": y, "z": z}
        (
            self.got, self.p0, self.p1, self.fl, self.fr,
            self.total2, self.q0, self.q1, self.gl, self.gr, self.total3, self.last,
        ) = scratch
        self.dims2 = without(self.DIMS, axes[0])
        self.dims3 = without(self.dims2, axes[1])

    @classmethod
    def scratch(cls, rows, axes):
        buf = lambda *lead: pltpu.VMEM(lead + (rows, 128), BF16)
        two = without(cls.DIMS, axes[0])
        three = without(two, axes[1])
        a, b = sizes(two), sizes(three)
        half_a, half_b = (a[0] // 2,) + a[1:], (b[0] // 2,) + b[1:]
        return (
            [buf(*sizes(cls.DIMS)), buf(*half_a), buf(*half_a), buf(*a), buf(*a)]
            + [buf(*a), buf(*half_b), buf(*half_b), buf(*b), buf(*b)]
            + [buf(*b), buf(3)]
        )

    def mine(self, i, core):
        return pick(self.source, self.DIMS, self.axes[0], i, core)[0]

    def block(self, i):
        return pick(self.got, self.DIMS, self.axes[0], i)[0]

    def block2(self, i):
        return pick(self.total2, self.dims2, self.axes[1], i)[0]

    def block3(self, i):
        return pick(self.total3, self.dims3, self.axes[2], i)[0]

    def swap(self):
        me = self.me[self.axes[0]]
        self.swaps = [
            self.links.send(self.mine(i, 1 - self.core), self.block(i), sibling())
            for i in ((me + 2) % 4, (me + 1) % 4, (me + 3) % 4, me)
        ]
        self.pending = list(self.swaps)

    def ready(self, i):
        self.pending.pop(0).wait_recv()
        add_into(self.block(i), self.mine(i, self.core))

    def start(self):
        first, second, third = self.axes
        self.ring = SumRing(
            self.links, first, self.me[first], self.block,
            lambda i, k: first_half(self.block(i), k),
            self.p0, self.p1, self.fl, self.fr, first_half,
        )
        self.ring2 = SumRing(
            self.links, second, self.me[second], self.block2,
            lambda i, k: first_half(self.block2(i), k),
            self.q0, self.q1, self.gl, self.gr, first_half,
        )
        self.direct = Direct(self.links, third, self.me[third], self.block3, self.last)
        self.ring.start(self.ready)

    def relay(self):
        self.ring.relay()

    def next(self):
        self.ring.finish(self.total2)
        self.ring2.start(nothing)

    def relay2(self):
        self.ring2.relay()

    def next2(self):
        self.ring2.finish(self.total3)
        self.direct.start()

    def finish(self):
        self.direct.finish(self.out)

    def drain(self):
        self.ring.drain()
        self.ring2.drain()
        self.direct.drain()
        for copy in self.swaps:
            copy.wait_send()


def tile(ref, inverse, step):
    parts = []
    for j in range(8):
        block = step * 8 + j
        late = block >= 64
        owner = inverse[jnp.where(late, 127 - block, block)]
        half = pl.multiple_of(jnp.where(late, 64, 0), 64)
        parts.append(ref[owner, pl.ds(half, 64), :])
    return jnp.concatenate(parts, axis=0)


def attend(own, inverse, query, keys, values, acc, weight):
    acc[...] = jnp.zeros_like(acc)
    weight[...] = jnp.zeros_like(weight)

    def step_for(part, block, step, masked):
        here = pl.ds(part * 256, 256)
        k = tile(keys, inverse, step)
        v = tile(values, inverse, step)
        raw = lax.dot_general(query[here, :], k, NT, preferred_element_type=F32)
        p = jnp.exp2(raw * EXP2_SCALE)
        if masked:
            token = lax.broadcasted_iota(jnp.int32, (256, 512), 0) % 64 + block * 64
            position = lax.broadcasted_iota(jnp.int32, (256, 512), 1) + step * 512
            p = jnp.where(position <= token, p, 0.0)
        weight[here, :] += p[:, :128] + p[:, 128:256] + p[:, 256:384] + p[:, 384:]
        acc[here, :] += jnp.dot(p.astype(BF16), v, preferred_element_type=F32)

    for part in range(2):
        block = own if part == 0 else 127 - own
        full = block // 8

        @pl.loop(0, full)
        def _(step):
            step_for(part, block, step, False)

        step_for(part, block, full, True)


def attend_back(own, inverse, query, d_out, log_sum, delta, keys, values, d_query, d_keys, d_values):
    d_query[...] = jnp.zeros_like(d_query)

    def terms(part, step, k, v, masked):
        rows = pl.ds(part * 256, 256)
        block = own if part == 0 else 127 - own
        q = query[rows, :]
        g = d_out[rows, :]
        raw = lax.dot_general(k, q, NT, preferred_element_type=F32)
        p = jnp.exp2(raw * EXP2_SCALE - log_sum[:, part * 256 : (part + 1) * 256])
        if masked:
            position = lax.broadcasted_iota(jnp.int32, (512, 256), 0) + step * 512
            token = lax.broadcasted_iota(jnp.int32, (512, 256), 1) % 64 + block * 64
            p = jnp.where(position <= token, p, 0.0)
        d_p = lax.dot_general(v, g, NT, preferred_element_type=F32)
        d_s = (p * (d_p - delta[:, part * 256 : (part + 1) * 256])).astype(BF16)
        d_query[rows, :] += lax.dot_general(d_s, k, TN, preferred_element_type=F32)
        d_k = jnp.dot(d_s, q, preferred_element_type=F32)
        d_v = jnp.dot(p.astype(BF16), g, preferred_element_type=F32)
        return d_k, d_v

    def store(step, d_k, d_v):
        for j in range(8):
            block = step * 8 + j
            late = block >= 64
            owner = inverse[jnp.where(late, 127 - block, block)]
            half = pl.multiple_of(jnp.where(late, 64, 0), 64)
            d_keys[owner, pl.ds(half, 64), :] = (d_k[j * 64 : (j + 1) * 64] * SCALE).astype(BF16)
            d_values[owner, pl.ds(half, 64), :] = d_v[j * 64 : (j + 1) * 64].astype(BF16)

    early_full = own // 8
    late_full = (127 - own) // 8

    @pl.loop(0, early_full)
    def _(step):
        k = tile(keys, inverse, step)
        v = tile(values, inverse, step)
        d_k, d_v = terms(1, step, k, v, False)
        d_k2, d_v2 = terms(0, step, k, v, False)
        store(step, d_k + d_k2, d_v + d_v2)

    k = tile(keys, inverse, early_full)
    v = tile(values, inverse, early_full)
    d_k, d_v = terms(1, early_full, k, v, False)
    d_k2, d_v2 = terms(0, early_full, k, v, True)
    store(early_full, d_k + d_k2, d_v + d_v2)

    @pl.loop(early_full + 1, late_full)
    def _(step):
        d_k, d_v = terms(1, step, tile(keys, inverse, step), tile(values, inverse, step), False)
        store(step, d_k, d_v)

    d_k, d_v = terms(
        1, late_full, tile(keys, inverse, late_full), tile(values, inverse, late_full), True
    )
    store(late_full, d_k, d_v)
    zero = jnp.zeros((512, 256), F32)

    @pl.loop(late_full + 1, 16)
    def _(step):
        store(step, zero, zero)

    d_query[...] = d_query[...] * SCALE


def dot(a, b):
    return jnp.dot(a, b, preferred_element_type=F32)


def dot_nt(a, b):
    return lax.dot_general(a, b, NT, preferred_element_type=F32)


def dot_tn(a, b):
    return lax.dot_general(a, b, TN, preferred_element_type=F32)


def norm_back(values, gain, d_out):
    r = lax.rsqrt(jnp.mean(values * values, axis=-1, keepdims=True) + EPS)
    n = values * r
    d_gain = jnp.sum(d_out * n, axis=0, keepdims=True)
    d_n = d_out * gain
    return r * (d_n - n * jnp.mean(d_n * n, axis=-1, keepdims=True)), d_gain


def gelu_terms(x):
    c = math.sqrt(2.0 / math.pi)
    square = x * x
    t = jnp.tanh(c * x * (1.0 + 0.044715 * square))
    half = 0.5 * (1.0 + t)
    slope = half + 0.5 * x * (1.0 - t * t) * c * (1.0 + 3 * 0.044715 * square)
    return x * half, slope


def by_fives(act):
    i = lax.broadcasted_iota(jnp.int32, (640, 640), 0)
    j = lax.broadcasted_iota(jnp.int32, (640, 640), 1)
    chosen = (i == 5 * (j % 128) + j // 128).astype(F32).astype(BF16)
    return dot(act, chosen).astype(BF16)


def spread_rows(flat, act, grad, rows, first=0, count=128):
    tiles = grad.shape[1] // 128
    for t in range(5):
        part = dot_tn(act[:, t * 128 + first : t * 128 + first + count], grad)
        for c in range(tiles):
            flat[pl.ds(t * tiles + c, count, stride=rows), :] = part[:, c * 128 : (c + 1) * 128]


def middle_kernel(
    inverse, pair, query, keys, values, inputs, cotangent, wo, wg, wu, wd, gains,
    layer_out, grad_resid_out, d_query, d_keys, d_values, act_two_out, hidden, d_down_out, d_gate, d_upper, att,
    d_att_out, gr_gains, acc, weight, gate, upper, d_att_rows,
):
    own = pair[0]
    attend(own, inverse, query, keys, values, acc, weight)
    attended = acc[...] / jnp.sum(weight[...], axis=1, keepdims=True)
    acc[...] = attended
    ones = jnp.ones((8, 128), F32)
    sums = lax.dot_general(
        ones, weight[...], NT, precision=lax.Precision.HIGHEST, preferred_element_type=F32
    )
    log_sum = jnp.log2(sums[:1])
    attended = attended.astype(BF16)
    for b in range(2):
        for head in range(4):
            att[b * 64 : (b + 1) * 64, head * 256 : (head + 1) * 256] = attended[
                b * 256 + head * 64 : b * 256 + (head + 1) * 64
            ]

    att_lin = dot(att[...], wo[...])
    resid = inputs[...].astype(F32) + norm_scale(att_lin, gain_row(gains, "post_attn"))
    act_two = norm_scale(resid, gain_row(gains, "pre_ff")).astype(BF16)
    act_two_out[...] = act_two
    for c in range(4):
        s = slice(c * 512, (c + 1) * 512)
        gate[:, s] = dot(act_two, wg[:, s])
        upper[:, s] = dot(act_two, wu[:, s])
        hidden[:, s] = (gelu_terms(gate[:, s])[0] * upper[:, s]).astype(BF16)
    down = dot(hidden[...], wd[...])
    layer_out[...] = (resid + norm_scale(down, gain_row(gains, "post_ff"))).astype(BF16)

    grad_y = cotangent[...].astype(F32)
    d_down, d_post_ff = norm_back(down, gain_row(gains, "post_ff"), grad_y)
    d_down = d_down.astype(BF16)
    d_down_out[...] = d_down
    d_act_two = jnp.zeros((128, 640), F32)
    for c in range(4):
        s = slice(c * 512, (c + 1) * 512)
        d_hidden = dot_nt(d_down, wd[s, :])
        value, slope = gelu_terms(gate[:, s])
        a = (d_hidden * upper[:, s] * slope).astype(BF16)
        b = (d_hidden * value).astype(BF16)
        d_gate[:, s] = a
        d_upper[:, s] = b
        d_act_two = d_act_two + dot_nt(a, wg[:, s]) + dot_nt(b, wu[:, s])
    d_resid, d_pre_ff = norm_back(resid, gain_row(gains, "pre_ff"), d_act_two)
    grad_resid = grad_y + d_resid
    grad_resid_out[...] = grad_resid
    d_att, d_post_attn = norm_back(att_lin, gain_row(gains, "post_attn"), grad_resid)
    d_att = d_att.astype(BF16)
    d_att_out[...] = d_att
    gr_gains[...] = jnp.concatenate(
        [d_post_attn, d_pre_ff, d_post_ff, jnp.zeros((5, 640), F32)], axis=0
    )
    d_attended = dot_nt(d_att, wo[...]).astype(BF16)
    for b in range(2):
        for head in range(4):
            d_att_rows[b * 256 + head * 64 : b * 256 + (head + 1) * 64] = d_attended[
                b * 64 : (b + 1) * 64, head * 256 : (head + 1) * 256
            ]
    delta = lax.dot_general(
        jnp.ones((8, 256), F32),
        d_att_rows[...].astype(F32) * acc[...],
        NT,
        precision=lax.Precision.HIGHEST,
        preferred_element_type=F32,
    )[:1]

    attend_back(
        own, inverse, query, d_att_rows, log_sum, delta, keys, values, d_query, d_keys, d_values
    )


def middle(*args):
    kv = pltpu.VMEM((64, 128, 256), BF16)
    act = lambda width: jax.ShapeDtypeStruct((128, width), BF16)
    return pl.pallas_call(
        middle_kernel,
        name="middle",
        out_shape=(
            act(640),
            jax.ShapeDtypeStruct((128, 640), F32),
            jax.ShapeDtypeStruct((512, 256), F32),
            kv, kv, act(640), act(2048), act(640), act(2048), act(2048), act(1024), act(640),
            jax.ShapeDtypeStruct((8, 640), F32),
        ),
        in_specs=[SMEM, SMEM] + [VMEM] * 10,
        out_specs=(VMEM,) * 13,
        scratch_shapes=[
            pltpu.VMEM((512, 256), F32),
            pltpu.VMEM((512, 128), F32),
            pltpu.VMEM((128, 2048), F32),
            pltpu.VMEM((128, 2048), F32),
            pltpu.VMEM((512, 256), BF16),
        ],
        compiler_params=pltpu.CompilerParams(vmem_limit_bytes=16 << 20),
    )(*args)


FIRST_ROWS, FIRST_ORDERS = (80, 40, 80, 80, 40), ("xyz", "zxy", "xzy", "yzx", "xyz")
LAST_ROWS, LAST_ORDERS = (16, 16), ("yzx", "zxy")


def spot(i):
    return (i // 64, (i // 16) % 4, (i // 4) % 4, (i // 2) % 2, i % 2)


def pack_places(out, flat, rows, first=0, size=None, start=0, count=128):
    @pl.loop(0, count // 4)
    def _(block):
        for j in range(4):
            i = block * 4 + j
            out[spot(start + i)] = flat[
                pl.ds(pl.multiple_of(i * rows + first, 8), size or rows), :
            ].astype(BF16)


def cut_by_fives(out, flat, act, grad):
    for start in (0, 64):
        spread_rows(flat, act, grad, 80, start, 64)
        pack_places(out, flat, 80, start=start, count=64)


def by_sixteens(out, act, grad):
    @pl.loop(0, 16)
    def _(i):
        part = dot_tn(act[:, pl.ds(pl.multiple_of(i * 128, 128), 128)], grad).astype(BF16)
        for j in range(8):
            for c in range(5):
                out[spot(i * 8 + j) + (pl.ds(c * 16, 16),)] = part[
                    j * 16 : (j + 1) * 16, c * 128 : (c + 1) * 128
                ]


def by_eights(out, act, grad):
    @pl.loop(0, 8)
    def _(i):
        part = dot_tn(act[:, pl.ds(pl.multiple_of(i * 128, 128), 128)], grad)
        for j in range(16):
            rows = part[j * 8 : (j + 1) * 8]
            out[spot(i * 16 + j)] = jnp.concatenate(
                [rows[:, c * 128 : (c + 1) * 128] for c in range(5)], axis=0
            ).astype(BF16)


class DirectSum:
    SCRATCH = 6
    DIMS = WeightSum.DIMS

    def __init__(self, links, source, out, scratch, axes):
        h, xl, z, y, core = place()
        self.links, self.source, self.out, self.axes = links, source, out, axes
        self.core, self.me = core, {"x": 2 * h + xl, "y": y, "z": z}
        self.total, self.last = scratch[:3], scratch[3:]
        self.dims = [self.DIMS]
        for axis in axes:
            self.dims.append(without(self.dims[-1], axis))

    @classmethod
    def scratch(cls, rows, axes):
        buf = lambda *lead: pltpu.VMEM(lead + (rows, 128), BF16)
        two = without(cls.DIMS, axes[0])
        three = without(two, axes[1])
        a, b = sizes(two), sizes(three)
        return [buf(*sizes(cls.DIMS)), buf(*a), buf(*b), buf(3, *a), buf(3, *b), buf(3)]

    def swap(self):
        self.copy = self.links.send(
            self.source.at[:, :, :, 1 - self.core], self.total[0], sibling()
        )

    def start(self):
        self.copy.wait_recv()
        add_into(self.total[0], self.source.at[:, :, :, self.core])
        self.stages = []
        self.send()

    def send(self):
        n = len(self.stages)
        axis = self.axes[n]
        stage = Direct(
            self.links, axis, self.me[axis],
            lambda i: pick(self.total[n], self.dims[n], axis, i)[0], self.last[n],
        )
        stage.start()
        self.stages.append(stage)

    def next(self):
        self.stages[-1].finish(self.total[len(self.stages)])
        self.send()

    def finish(self):
        self.stages[-1].finish(self.out)

    def drain(self):
        for stage in self.stages:
            stage.drain()
        self.copy.wait_send()


def project_back(
    d_query, d_key, d_value, query_lin, key_lin, act_one, inputs, wq, wkv, gains, cosine, sine, grad_resid, d_gains,
    input_grad, gr_query, gr_tail,
    d_query_lin, d_kv_lin, flat,
):
    cos, sin = cosine[...], sine[...]

    def turn_back(lin, gain, grad):
        a, b = grad[:, :128], grad[:, 128:]
        d_n = jnp.concatenate([a * cos + b * sin, b * cos - a * sin], axis=1)
        return norm_back(lin, gain, d_n)

    fives = by_fives(act_one[...])
    d_gain_query = jnp.zeros((1, 256), F32)
    for head in range(4):
        cut = slice(head * 256, (head + 1) * 256)
        grad = jnp.concatenate(
            [d_query[b * 256 + head * 64 : b * 256 + (head + 1) * 64] for b in range(2)], axis=0
        )
        d_lin, d_gain = turn_back(query_lin[:, cut], gain_row(gains, "query"), grad)
        d_query_lin[:, cut] = d_lin.astype(BF16)
        d_gain_query = d_gain_query + d_gain
    spread_rows(flat, fives, d_query_lin[...], 40)
    pack_places(gr_query, flat, 40)
    d_act = dot_nt(d_query_lin[...], wq[...])
    yield
    d_lin, d_gain_key = turn_back(key_lin[...], gain_row(gains, "key"), d_key[...])
    d_kv_lin[:, :256] = d_lin.astype(BF16)
    d_kv_lin[:, 256:] = d_value[...].astype(BF16)
    d_act = d_act + dot_nt(d_kv_lin[...], wkv[...])
    d_states, d_gain_in = norm_back(inputs[...].astype(F32), gain_row(gains, "in"), d_act)
    input_grad[...] = (grad_resid[...] + d_states).astype(BF16)
    for row in range(21, 32):
        flat[pl.ds(row, 128, stride=32), :] = jnp.zeros((128, 128), F32)
    spread_rows(flat, fives, d_kv_lin[...], 32)
    total = jnp.zeros((128, 128), F32)
    column = 0
    for row, each in (
        (d_gain_in, 5),
        (d_gains[0:1], 5),
        (d_gains[1:2], 5),
        (d_gains[2:3], 5),
        (d_gain_query, 2),
        (d_gain_key, 2),
    ):
        n = 128 * each
        owner = lax.broadcasted_iota(jnp.int32, (128, n), 1) // each
        mine = owner == lax.broadcasted_iota(jnp.int32, (128, n), 0)
        where = lax.broadcasted_iota(jnp.int32, (n, 128), 0) % each + column
        here = where == lax.broadcasted_iota(jnp.int32, (n, 128), 1)
        total = total + dot(
            jnp.where(mine, row, 0.0).astype(BF16), here.astype(F32).astype(BF16)
        )
        column += each
    flat[pl.ds(20, 128, stride=32), :] = total
    for k in range(2):
        pack_places(gr_tail[k], flat, 32, 16 * k, 16)
    yield


def back_kernel(*refs):
    refs = list(refs)

    def take(n):
        some = refs[:n]
        del refs[:n]
        return some

    kv_sources, acts, others = take(2), take(7), take(12)
    input_grad, o_query, o_key, o_value, o_output, o_gate, o_up, o_down, o_gains = take(9)
    kv_sums = take(2)
    first_sums, last_sums = take(5), take(2)
    first_sources, last_sources = take(5), take(2)
    d_query_lin, d_kv_lin, flat = take(3)
    kv_scratch = [take(KeySum.SCRATCH) for _ in range(2)]
    first_scratch = [take(WeightSum.SCRATCH) for _ in range(5)]
    last_scratch = [take(DirectSum.SCRATCH) for _ in range(2)]
    send_sems, recv_sems = refs
    greet(
        [sibling()] + [axis_neighbour(a, s) for a in ("x", "y", "z") for s in (1, 2, 3)]
    )
    links = Links(send_sems, recv_sems)
    kv = [
        KeySum(links, *args)
        for args in zip(kv_sources, kv_sums, kv_scratch, ("zy", "yz"))
    ]
    first = [
        WeightSum(links, *args)
        for args in zip(first_sources, first_sums, first_scratch, FIRST_ORDERS)
    ]
    final = [
        DirectSum(links, *args)
        for args in zip(last_sources, last_sums, last_scratch, LAST_ORDERS)
    ]
    down, output, gate, up, query = first
    act_two, hidden, d_down, d_gate, d_upper, att, d_att = acts
    projections = project_back(
        others[0], *kv_sums, *others[1:], input_grad, first_sources[4], last_sources,
        d_query_lin, d_kv_lin, flat,
    )

    def run(group, *stages):
        for stage in stages:
            for s in group:
                getattr(s, stage)()

    run(kv, "swap", "start")
    by_sixteens(first_sources[0], hidden, d_down[...])
    down.swap()
    run(kv, "relay")
    by_eights(first_sources[1], att, d_att[...])
    output.swap()
    down.start()
    output.start()
    fives = by_fives(act_two[...])
    cut_by_fives(first_sources[2], flat, fives, d_gate[...])
    gate.swap()
    run(kv, "next")
    down.relay()
    output.relay()
    gate.start()
    run(kv, "relay2")
    cut_by_fives(first_sources[3], flat, fives, d_upper[...])
    up.swap()
    run(kv, "next2")
    up.start()
    down.next()
    output.next()
    next(projections)
    query.swap()
    run(kv, "finish")
    next(projections)
    run(final, "swap")
    query.start()
    run(final, "start")
    gate.relay()
    up.relay()
    query.relay()
    run(final, "next")
    run([down, output], "relay2")
    run([gate, up, query], "next")
    run(final, "next")
    run([down, output], "next2")
    run([gate, up, query], "relay2", "next2")
    run(final, "finish")
    run(first, "finish")
    run(kv + first + final, "drain")

    s_down, s_output, s_gate, s_up, s_query = first_sums
    s_tail = jnp.concatenate([part[...] for part in last_sums], axis=0)
    for c in range(5):
        cut = slice(c * 128, (c + 1) * 128)
        o_down[:, cut] = s_down[c * 16 : (c + 1) * 16, :]
        o_output[:, cut] = s_output[c * 8 : (c + 1) * 8, :]
    for out, source, step in ((o_gate, s_gate, 16), (o_up, s_up, 16), (o_query, s_query, 8)):
        for c in range(step):
            out[:, c * 128 : (c + 1) * 128] = source[pl.ds(c, 5, stride=step), :]
    for t in range(5):
        for c in range(2):
            cut = slice(c * 128, (c + 1) * 128)
            o_key[t : t + 1, cut] = s_tail[t * 4 + c : t * 4 + c + 1]
            o_value[t : t + 1, cut] = s_tail[t * 4 + c + 2 : t * 4 + c + 3]
    o_gains[...] = s_tail[20:21]


def back(kv, acts, others):
    buf = lambda *shape: pltpu.VMEM(shape, F32)
    scratch = [buf(128, 256)] * 2
    scratch += [buf(rows, 128) for rows in FIRST_ROWS + LAST_ROWS]
    scratch += [pltpu.VMEM((2, 4, 4, 2, 2, rows, 128), BF16) for rows in FIRST_ROWS + LAST_ROWS]
    scratch += [
        pltpu.VMEM((128, 1024), BF16),
        pltpu.VMEM((128, 512), BF16),
        buf(64 * 80, 128),
    ]
    for _ in kv:
        scratch += KeySum.scratch()
    for rows, order in zip(FIRST_ROWS, FIRST_ORDERS):
        scratch += WeightSum.scratch(rows, order)
    for rows, order in zip(LAST_ROWS, LAST_ORDERS):
        scratch += DirectSum.scratch(rows, order)
    count = 2 * 17 + 5 * 19 + 2 * 10
    out = lambda rows, width: jax.ShapeDtypeStruct((rows, width), F32)
    return pl.pallas_call(
        back_kernel,
        name="back",
        out_shape=(
            jax.ShapeDtypeStruct((128, 640), BF16),
            out(5, 1024), out(5, 256), out(5, 256), out(8, 640), out(5, 2048), out(5, 2048),
            out(16, 640), out(1, 128),
        ),
        in_specs=[VMEM] * 21,
        out_specs=(VMEM,) * 9,
        scratch_shapes=scratch
        + [pltpu.SemaphoreType.DMA((count,)), pltpu.SemaphoreType.DMA((count,))],
        compiler_params=pltpu.CompilerParams(
            collective_id=2, has_side_effects=True, vmem_limit_bytes=47 << 20
        ),
    )(
        *[g.reshape((2, 4, 4, 2) + g.shape[1:]) for g in kv],
        *acts,
        *others,
    )


def local(
    inputs,
    pair_order,
    w_query,
    w_key,
    w_value,
    w_output,
    w_gate,
    w_up,
    w_down,
    gain_in,
    gain_query,
    gain_key,
    gain_post_attn,
    gain_pre_ff,
    gain_post_ff,
    cotangent,
):
    rows = 128
    me_index = lax.axis_index("ctx")
    own_pair = lax.dynamic_slice_in_dim(pair_order, me_index, 1)
    within = jnp.arange(rows, dtype=jnp.int32)
    block_id = jnp.where(within < 64, own_pair, 127 - own_pair)
    positions = block_id * 64 + within % 64
    freq = ROPE_BASE ** (-jnp.arange(128, dtype=F32) / 128)
    angles = positions.astype(F32)[:, None] * freq
    cosine, sine = jnp.cos(angles), jnp.sin(angles)
    matches = pair_order[None, :] == jnp.arange(64, dtype=jnp.int32)[:, None]
    inverse = jnp.sum(jnp.where(matches, jnp.arange(64, dtype=jnp.int32)[None, :], 0), axis=1)
    gains, first = jnp.zeros((3072,), F32), 0
    for g in (gain_in, gain_post_attn, gain_pre_ff, gain_post_ff, gain_query, gain_key):
        gains = gains + jnp.pad(g, (first, 3072 - first - g.shape[0]))
        first += g.shape[0]
    gains = gains.reshape(24, 128)
    (
        wq_all, wkv_all, wo_all, wg_all, wu_all, wd_all, keys, values,
        act_one, query_lin, key_lin, query,
    ) = front(
        (w_query, w_key, w_value, w_output, w_gate, w_up, w_down), inputs[0], gains, cosine, sine
    )
    (
        layer_out, grad_resid, d_query, d_keys, d_values, act_two, hidden, d_down, d_gate, d_upper, att, d_att,
        d_gains,
    ) = middle(
        inverse, own_pair, query, keys, values, inputs[0], cotangent[0],
        wo_all, wg_all, wu_all, wd_all, gains,
    )
    input_grad, s_query, s_key, s_value, s_output, s_gate, s_up, s_down, s_gains = back(
        (d_keys, d_values), (act_two, hidden, d_down, d_gate, d_upper, att, d_att),
        (d_query, query_lin, key_lin, act_one, inputs[0], wq_all, wkv_all, gains, cosine, sine, grad_resid, d_gains),
    )
    s_gains = s_gains[0]
    return (
        layer_out[None],
        input_grad[None],
        s_query,
        s_key,
        s_value,
        s_output,
        s_gate,
        s_up,
        s_down,
        s_gains[0:5],
        s_gains[20:22],
        s_gains[22:24],
        s_gains[5:10],
        s_gains[10:15],
        s_gains[15:20],
    )


def solution(mesh):
    placed = (
        P("fsdp", "ctx", None),
        P(),
        P("fsdp", None),
        P("fsdp", None),
        P("fsdp", None),
        P("fsdp", None),
        P("fsdp", None),
        P("fsdp", None),
        P("fsdp", None),
        P(),
        P(),
        P(),
        P(),
        P(),
        P(),
        P("fsdp", "ctx", None),
    )
    both = ("ctx", "fsdp")
    return jax.shard_map(
        local,
        mesh=mesh,
        in_specs=placed,
        out_specs=(P("fsdp", "ctx", None),) * 2 + (P(both, None),) * 7 + (P(both),) * 6,
        check_vma=False,
    )
```
